32 devices in a mesh: dp: 4 (over z), ctx: 8 (over y, x, core).
Axes of the slice: x: 2, y: 2, z: 4, core: 2. Of those that a mesh axis runs over, the one named last changes fastest.
Arguments:
- inputs: bfloat16 [4, 131072, 256], P('dp', 'ctx'), may hold values from -6 to 6
- grad_out: bfloat16 [4, 131072, 256], P('dp', 'ctx'), may hold values from -6 to 6
- w_in: bfloat16 [256, 768], replicated, may hold values from -0.375 to 0.375
- filter_real: float32 [512, 512, 16], P('ctx'), may hold values from -12 to 12, as said below
- filter_imag: float32 [512, 512, 16], P('ctx'), may hold values from -12 to 12, as said below
Outputs:
- gated_out: bfloat16 [4, 131072, 256], P('dp', 'ctx')
- grad_w_in: float32 [256, 768], P('dp')
The draws below stay inside these ranges and needn't reach their ends.
Inputs may be any that keep to these rules, and one draw needn't show every extreme that they name: Each long filter is real: with P = 262144, filter_real at frequency (P - f) mod P equals filter_real at frequency f. Each long filter is real: with P = 262144, filter_imag at frequency (P - f) mod P is minus filter_imag at frequency f.
All inputs are finite; a program needn't handle non-finite values.
Results may differ from the reference program's by a relative error of at most 0.011.
Values may be sent and summed in bfloat16 or wider, within the bound.
No kernel may reach another device: no remote copies, remote signals or barrier semaphores. Data moves between devices by JAX's collectives and lax.ppermute only.
A program may use at most 384 MiB of HBM per device.

```python
import math
import jax
import jax.numpy as jnp
from jax import lax

C = 256
N1 = 512
N2 = 512
FG = 16
BATCH = 4
SEQ = 131072


def spectrum_pair(key):
    base_key = jax.random.fold_in(key, 31)
    real_key, imag_key = jax.random.split(base_key, 2)
    shape_three = (N1, N2, FG)
    real_noise = jax.random.truncated_normal(real_key, -4.0, 4.0, shape_three, jnp.float32)
    imag_noise = jax.random.truncated_normal(imag_key, -4.0, 4.0, shape_three, jnp.float32)
    row_index = jnp.arange(N1, dtype=jnp.int32)
    col_index = jnp.arange(N2, dtype=jnp.int32)
    mirror_row = (N1 - row_index) % N1
    mirror_col = (N2 - col_index[None, :] - (row_index[:, None] > 0).astype(jnp.int32)) % N2
    mirror_real = real_noise[mirror_row[:, None], mirror_col]
    mirror_imag = imag_noise[mirror_row[:, None], mirror_col]
    half_root = math.sqrt(0.5)
    spec_real = (real_noise + mirror_real) * half_root
    spec_imag = (imag_noise - mirror_imag) * half_root
    return (spec_real.astype(jnp.float32), spec_imag.astype(jnp.float32))


def draw_filter_real(key, part):
    return spectrum_pair(key)[0]


def draw_filter_imag(key, part):
    return spectrum_pair(key)[1]


def raised(values, rng, source, target, shards_of, factor):
    owner, partner = [(jnp.arange(values.shape[axis_at]) // (values.shape[axis_at] // shards_of)).reshape([-1 if axis == axis_at else 1 for axis in range(values.ndim)]) for axis_at in (source, target)]
    chosen = jax.random.permutation(rng, shards_of)[partner]
    strong = (owner == chosen) | (owner == (partner + shards_of // 2) % shards_of)
    return jnp.where(strong, factor * values, values)


def block_levels(stream_key, shape, shards, smallest, largest):
    gain, own = 1.0, jax.random.fold_in(stream_key, 6)
    for position, parts in shards:
        draws = jnp.exp(jax.random.uniform(jax.random.fold_in(own, position), (parts,), jnp.float32, smallest / len(shards), largest / len(shards)))
        gain = gain * jnp.repeat(draws, shape[position] // parts).reshape([-1 if axis == position else 1 for axis in range(len(shape))])
    return gain


def bell_draw(stream_key, extent, deviation, most, pieces=(), kind=jnp.bfloat16):
    factor_of = block_levels(stream_key, extent, pieces, -0.22, 0.18) if pieces else 1.0
    values = jax.random.normal(stream_key, extent, jnp.float32) * deviation * factor_of
    return jnp.minimum(jnp.maximum(values, -most), most).astype(kind)


def bell_draw_with(stream_key, extent, scale, bound, cuts, heavy, kind=jnp.bfloat16):
    entries = scale * jax.random.normal(stream_key, extent, jnp.float32)
    if cuts:
        entries = entries * block_levels(stream_key, extent, cuts, -0.22, 0.18)
    return jnp.clip(raised(entries, jax.random.fold_in(stream_key, 3), *heavy), -bound, bound).astype(kind)


def setup_inputs(seed: int = 0) -> dict:
    arg_keys = jax.random.split(jax.random.key(seed), 6)
    return {
        "inputs": bell_draw_with(arg_keys[0], (BATCH, SEQ, C), 1.0, 6.0, ((0, 4), (1, 8)), (1, 2, 8, 2.0)),
        "grad_out": bell_draw(arg_keys[1], (BATCH, SEQ, C), 1.0, 6.0, ((0, 4), (1, 8))),
        "w_in": bell_draw(arg_keys[2], (C, 3 * C), C ** -0.5, 0.375),
        "filter_real": draw_filter_real(jax.random.fold_in(arg_keys[5], 71), 0),
        "filter_imag": draw_filter_imag(jax.random.fold_in(arg_keys[5], 71), 0),
    }


def widen(array_value):
    return lax.optimization_barrier(array_value).astype(jnp.float32)

def dft_tables(row_index, col_index, period, factor):
    phase_angle = (row_index[:, None] * col_index[None, :] % period).astype(jnp.float32) * (2.0 * math.pi / period)
    return ((jnp.cos(phase_angle) * factor).astype(jnp.bfloat16), (jnp.sin(phase_angle) * factor).astype(jnp.bfloat16))

def twiddle_tables(row_index, col_index, period):
    phase_angle = (row_index[:, None] * col_index[None, :] % period).astype(jnp.float32) * (2.0 * math.pi / period)
    return (jnp.cos(phase_angle)[:, :, None], jnp.sin(phase_angle)[:, :, None])

def combine(cos_part, sin_part, orient):
    real_part = cos_part[:, :, 0] - orient * sin_part[:, :, 1]
    imag_part = cos_part[:, :, 1] + orient * sin_part[:, :, 0]
    return (real_part, imag_part)

def rotate(real_part, imag_part, cos_table, sin_table, orient):
    new_real = real_part * cos_table - orient * imag_part * sin_table
    new_imag = imag_part * cos_table + orient * real_part * sin_table
    return (new_real, new_imag)

def pack_complex(real_part, imag_part):
    return jnp.stack([real_part, imag_part], axis=2).astype(jnp.bfloat16)

def long_conv(block_data, tables, filter_real, filter_imag):
    cos_one, sin_one, cos_two, sin_two, twist_cos, twist_sin = tables
    half_rows = cos_one.shape[1]
    shaped = widen(block_data).reshape(half_rows, cos_two.shape[0], 2, block_data.shape[-1])
    cos_part = jnp.einsum('ft,tcpm->fcpm', cos_one, shaped)
    sin_part = jnp.einsum('ft,tcpm->fcpm', sin_one, shaped)
    real_part, imag_part = combine(cos_part, sin_part, -1.0)
    real_part, imag_part = rotate(real_part, imag_part, twist_cos, twist_sin, -1.0)
    columns = widen(pack_complex(real_part, imag_part))
    cos_part = jnp.einsum('fcpm,cg->fgpm', columns, cos_two)
    sin_part = jnp.einsum('fcpm,cg->fgpm', columns, sin_two)
    real_part, imag_part = combine(cos_part, sin_part, -1.0)
    prod_real = real_part * filter_real - imag_part * filter_imag
    prod_imag = real_part * filter_imag + imag_part * filter_real
    product = widen(pack_complex(prod_real, prod_imag))
    cos_part = jnp.einsum('fgpm,gc->fcpm', product, cos_two)
    sin_part = jnp.einsum('fgpm,gc->fcpm', product, sin_two)
    real_part, imag_part = combine(cos_part, sin_part, 1.0)
    real_part, imag_part = rotate(real_part, imag_part, twist_cos, twist_sin, 1.0)
    returned = widen(pack_complex(real_part, imag_part))
    cos_part = jnp.einsum('ft,fcpm->tcpm', cos_one, returned)
    sin_part = jnp.einsum('ft,fcpm->tcpm', sin_one, returned)
    real_part, imag_part = combine(cos_part, sin_part, 1.0)
    return pack_complex(real_part, imag_part).reshape(block_data.shape)

def reference(inputs, grad_out, w_in, filter_real, filter_imag):
    seq_count, seq_len, chan_total = inputs.shape
    chan_half = chan_total // 2
    period = N1 * N2
    full_index = jnp.arange(N1, dtype=jnp.int32)
    half_index = jnp.arange(N1 // 2, dtype=jnp.int32)
    second_index = jnp.arange(N2, dtype=jnp.int32)
    cos_one, sin_one = dft_tables(full_index, half_index, N1, 1.0 / math.sqrt(N1))
    cos_two, sin_two = dft_tables(second_index, second_index, N2, 1.0 / math.sqrt(N2))
    twist_cos, twist_sin = twiddle_tables(full_index, second_index, period)
    tables = (widen(cos_one), widen(sin_one), widen(cos_two), widen(sin_two), twist_cos, twist_sin)
    filter_count = filter_real.shape[2]

    def conv_all(signal, orient):
        blocks = signal.reshape(seq_len, 2, chan_half // filter_count, filter_count).transpose(2, 0, 1, 3)

        def one_block(block_data):
            return long_conv(block_data, tables, filter_real, orient * filter_imag)
        result = lax.map(one_block, blocks)
        return result.transpose(1, 2, 0, 3).reshape(seq_len, chan_total)
    weight_total = jnp.zeros((chan_total, 3 * chan_total), jnp.float32)
    gated_list = []
    for seq_index in range(seq_count):
        tokens = inputs[seq_index]
        cotangent = widen(grad_out[seq_index])
        features = jnp.dot(widen(tokens), widen(w_in)).astype(jnp.bfloat16)
        wide_features = widen(features)
        gate_part = wide_features[:, :chan_total]
        key_part = wide_features[:, chan_total:2 * chan_total]
        value_part = wide_features[:, 2 * chan_total:]
        mixed = (key_part * value_part).astype(jnp.bfloat16)
        smooth = widen(conv_all(mixed, 1.0))
        gated_list.append((gate_part * smooth).astype(jnp.bfloat16))
        grad_smooth = (cotangent * gate_part).astype(jnp.bfloat16)
        grad_gate = (cotangent * smooth).astype(jnp.bfloat16)
        grad_mixed = widen(conv_all(grad_smooth, -1.0))
        grad_key = (grad_mixed * value_part).astype(jnp.bfloat16)
        grad_value = (grad_mixed * key_part).astype(jnp.bfloat16)
        grad_features = jnp.concatenate([grad_gate, grad_key, grad_value], axis=1)
        weight_total = weight_total + lax.dot_general(widen(tokens), widen(grad_features), (((0,), (0,)), ((), ())))
    grad_w_in = weight_total * (1.0 / math.sqrt(seq_count * seq_len))
    return (jnp.stack(gated_list, axis=0), grad_w_in)
```

```python
import functools
import math

import jax
import jax.numpy as jnp
import ml_dtypes
import numpy as np
from jax import lax
from jax.experimental import pallas as pl
from jax.experimental.pallas import tpu as pltpu
from jax.sharding import PartitionSpec as P

BF = jnp.bfloat16
F32 = jnp.float32
VMEM_BYTES = 60 * 1024 * 1024
POS_SPEC = pl.BlockSpec(memory_space=pltpu.SMEM)


def dot_nn(left, right):
    return lax.dot_general(left, right, (((1,), (0,)), ((), ())), preferred_element_type=F32)


def dot_nt(left, right):
    return lax.dot_general(left, right, (((1,), (1,)), ((), ())), preferred_element_type=F32)


def dot_tn(left, right):
    return lax.dot_general(left, right, (((0,), (0,)), ((), ())), preferred_element_type=F32)


def rounded(value):
    return value.astype(BF).astype(F32)


def transform_tables(n_one, n_two):
    def table(rows, cols, period):
        angle = (np.arange(rows)[:, None] * np.arange(cols)[None, :] % period) * (
            2.0 * math.pi / period
        )
        factor = 1.0 / math.sqrt(period)
        return (
            (np.cos(angle) * factor).astype(np.float32).astype(ml_dtypes.bfloat16),
            (np.sin(angle) * factor).astype(np.float32).astype(ml_dtypes.bfloat16),
        )

    cos_one, sin_one = table(n_one, n_one // 2, n_one)
    cos_two, sin_two = table(n_two, n_two, n_two)
    period = n_one * n_two
    angle = (np.arange(n_one)[:, None] * np.arange(n_two)[None, :] % period) * (
        2.0 * math.pi / period
    )
    first = np.block([[cos_one, sin_one], [-sin_one, cos_one]])
    second = np.block([[cos_two, -sin_two], [sin_two, cos_two]])
    third = np.block([[cos_two, sin_two], [-sin_two, cos_two]])
    fourth = np.block([[cos_one.T, -sin_one.T], [sin_one.T, cos_one.T]])
    return (
        first,
        second,
        third,
        fourth,
        np.cos(angle).astype(np.float32),
        np.sin(angle).astype(np.float32),
    )


def channel_order(chan_half, filters, ctx_count, chunks):
    repeats = chan_half // filters
    per_device = chan_half // ctx_count
    per_chunk = per_device // chunks
    order = []
    for chunk in range(chunks):
        for device in range(ctx_count):
            for part in range(2):
                for place in range(per_chunk):
                    index = device * per_device + chunk * per_chunk + place
                    group, repeat = divmod(index, repeats)
                    order.append(part * chan_half + repeat * filters + group)
    return np.array(order)


def gather_rows(pos_ref, pick_ref, held_ref, peers, blocks, rows):
    pos = pos_ref[0]
    chunks = pick_ref.shape[0] // (peers * rows)
    spot = 0
    for block in blocks:
        for chunk in range(chunks):
            start = pl.multiple_of((chunk * peers + (pos ^ block)) * rows, rows)
            held_ref[spot : spot + rows, :] = pick_ref[pl.ds(start, rows), :]
            spot += rows


def key_value_weights(w_ref, held_ref, wt_ref):
    count, chan = held_ref.shape
    for part in range(2):
        block = w_ref[:, (1 + part) * chan : (2 + part) * chan]
        wt_ref[part * count : (part + 1) * count, :] = dot_nt(held_ref[...], block).astype(BF)


def store_blocks(value, outs, step):
    chunks, _, rows, _ = outs[0].shape
    spot = 0
    for out in outs:
        for chunk in range(chunks):
            out[chunk, step] = value[spot : spot + rows]
            spot += rows


def load_blocks(parts, step):
    chunks = parts[0].shape[0]
    return jnp.concatenate(
        [part[chunk, step] for part in parts for chunk in range(chunks)], axis=0
    ).astype(F32)


def mixed_kernel(pos_ref, tok_ref, w_ref, pick_ref, *rest, peers, blocks):
    outs, (held_ref, wt_ref) = rest[:-2], rest[-2:]
    _, steps, rows, width = outs[0].shape
    count = held_ref.shape[0]

    @pl.when(pl.program_id(0) == 0)
    def _():
        gather_rows(pos_ref, pick_ref, held_ref, peers, blocks, rows)
        key_value_weights(w_ref, held_ref, wt_ref)

    for step in range(steps):
        feats = rounded(dot_nt(wt_ref[...], tok_ref[step * width : (step + 1) * width, :]))
        store_blocks((feats[:count] * feats[count:]).astype(BF), outs, step)


def grad_kernel(pos_ref, tok_ref, cot_ref, w_ref, pick_ref, *rest, peers):
    outs, (held_ref, wt_ref) = rest[:-2], rest[-2:]
    _, steps, rows, width = outs[0].shape
    chan = pick_ref.shape[1]

    @pl.when(pl.program_id(0) == 0)
    def _():
        gather_rows(pos_ref, pick_ref, held_ref, peers, range(peers), rows)
        wt_ref[...] = dot_nt(held_ref[...], w_ref[:, :chan]).astype(BF)

    for step in range(steps):
        span = slice(step * width, (step + 1) * width)
        gate = rounded(dot_nt(wt_ref[...], tok_ref[span, :]))
        cot = dot_nt(held_ref[...], cot_ref[span, :])
        store_blocks((gate * cot).astype(BF), outs, step)


def convolve(signal, refs, filt_real, filt_imag, orient, hold_ref):
    first_ref, second_ref, third_ref, fourth_ref, cos_ref, sin_ref = refs
    n_one = cos_ref.shape[0]
    n_two = cos_ref.shape[1]
    block = n_one // 2
    for start in range(0, n_one, block):
        span = slice(start, start + block)
        low = slice(n_one + start, n_one + start + block)
        cos, sin = cos_ref[span, :], sin_ref[span, :]
        real = dot_nn(first_ref[span, :], signal)
        imag = dot_nn(first_ref[low, :], signal)
        turned = jnp.concatenate(
            [(real * cos + imag * sin).astype(BF), (imag * cos - real * sin).astype(BF)], axis=1
        )
        spec = dot_nn(turned, second_ref[...])
        real, imag = spec[:, :n_two], spec[:, n_two:]
        f_real = filt_real(span).astype(F32)
        f_imag = filt_imag(span).astype(F32) * orient
        product = jnp.concatenate(
            [
                (real * f_real - imag * f_imag).astype(BF),
                (real * f_imag + imag * f_real).astype(BF),
            ],
            axis=1,
        )
        back = dot_nn(product, third_ref[...])
        real, imag = back[:, :n_two], back[:, n_two:]
        hold_ref[span, :] = (real * cos - imag * sin).astype(BF)
        hold_ref[low, :] = (imag * cos + real * sin).astype(BF)
    return dot_nn(fourth_ref[...], hold_ref[...])


def conv_kernel(pos_ref, *args, peers, rows, orient):
    ins, rest = args[:peers], args[peers:]
    tables, rest = rest[:6], rest[6:]
    parts_ref, rest = rest[0], rest[1:]
    outs, (in_ref, res_ref, hold_ref, filt_ref) = rest[-4 - peers : -4], rest[-4:]
    lanes = 128
    _, size, width = ins[0].shape
    times = peers * size // rows
    half = rows // 2
    place = pl.program_id(0)
    pos = pos_ref[0]
    piece = math.gcd(size, 256)

    @pl.when(place == 0)
    def _():
        groups, _, _, _, quarter, _ = parts_ref.shape
        for block in range(peers):
            base = (pos ^ block) * size
            for group in range(groups):
                start = (block * groups + group) * quarter
                span = slice(start, start + quarter)
                for part in range(2):
                    filt_ref[part, span, :] = parts_ref[group, block, 0, part]

            @pl.loop(0, size // piece)
            def _(index):
                wide = ins[block][0, pl.ds(pl.multiple_of(index * piece, piece), piece), :]
                wide = wide.astype(F32)
                span = pl.ds(pl.multiple_of(base + index * piece, piece), piece)
                for lane in range(width // lanes):
                    in_ref[lane, span, :] = wide[:, lane * lanes : (lane + 1) * lanes]

    parts = []
    for part in range(2):
        columns = [
            in_ref[lane, pl.ds(place + part * half, times, stride=rows), :].astype(BF)
            for lane in range(width // lanes)
        ]
        parts.append(jnp.concatenate(columns, axis=1))
    signal = jnp.concatenate(parts, axis=0)
    result = convolve(
        signal,
        tables,
        lambda span: filt_ref[0, span, :],
        lambda span: filt_ref[1, span, :],
        orient,
        hold_ref,
    )
    for part in range(2):
        for lane in range(width // lanes):
            res_ref[lane, pl.ds(place + part * half, times, stride=rows), :] = result[
                part * times : (part + 1) * times, lane * lanes : (lane + 1) * lanes
            ]

    @pl.when(place == pl.num_programs(0) - 1)
    def _():
        for block in range(peers):
            base = (pos ^ block) * size

            @pl.loop(0, size // piece)
            def _(index):
                span = pl.ds(pl.multiple_of(base + index * piece, piece), piece)
                outs[block][0, pl.ds(pl.multiple_of(index * piece, piece), piece), :] = (
                    jnp.concatenate(
                        [res_ref[lane, span, :] for lane in range(width // lanes)], axis=1
                    ).astype(BF)
                )


def conv_plain_kernel(x_ref, first, second, third, fourth, cos, sin, fr_ref, fi_ref, out_ref,
                      hold_ref, *, orient):
    out_ref[0] = convolve(
        x_ref[0],
        (first, second, third, fourth, cos, sin),
        lambda span: fr_ref[0, span, :],
        lambda span: fi_ref[0, span, :],
        orient,
        hold_ref,
    ).astype(BF)


def whole(shape):
    zeros = (0,) * len(shape)
    return pl.BlockSpec(shape, lambda *_: zeros, pipeline_mode=pl.Buffered(1))


def params():
    return pltpu.CompilerParams(
        dimension_semantics=("arbitrary",), vmem_limit_bytes=VMEM_BYTES
    )


def conv_cost(count, n_one, n_two, moved):
    macs = count * 2 * (n_one * n_one * n_two + 2 * n_one * n_two * n_two)
    return pl.CostEstimate(flops=2 * macs, bytes_accessed=moved, transcendentals=0)


def run_conv(blocks, tables, parts, chunk, repeats, orient, pos, joined):
    peers = len(blocks)
    chunks, size, width = blocks[0].shape
    n_one, n_two = tables[4].shape
    rows = size * peers // (n_one // 2)
    half = rows // 2
    table_specs = [whole(table.shape) for table in tables]
    block_spec = pl.BlockSpec(
        (1, size, width), lambda place: (chunk, 0, 0), pipeline_mode=pl.Buffered(1)
    )
    parts_shape = parts.shape[:2] + (1,) + parts.shape[3:]
    place_of = (0, 0, chunk * half // repeats, 0, 0, 0)
    parts_spec = pl.BlockSpec(
        parts_shape, lambda place: place_of, pipeline_mode=pl.Buffered(1)
    )
    moved = 4 * peers * size * width
    moved += sum(table.size * table.dtype.itemsize for table in tables)
    slots = pltpu.VMEM((width // 128, peers * size, 128), F32)
    first = 1 + peers + len(tables) + 1
    out_spec = pl.BlockSpec((1, size, width), lambda place: (chunk, 0, 0))
    return list(pl.pallas_call(
        functools.partial(conv_kernel, peers=peers, rows=rows, orient=orient),
        grid=(half,),
        in_specs=[POS_SPEC] + [block_spec] * peers + table_specs + [parts_spec]
        + [pl.BlockSpec(memory_space=pl.ANY)] * len(joined),
        out_specs=[out_spec] * peers,
        out_shape=[jax.ShapeDtypeStruct((chunks, size, width), BF)] * peers,
        input_output_aliases={first + index: index for index in range(len(joined))},
        scratch_shapes=[
            slots, slots, pltpu.VMEM((2 * n_one, n_two), BF), pltpu.VMEM((2, n_one, n_two), BF)
        ],
        compiler_params=params(),
        cost_estimate=conv_cost(half, n_one, n_two, moved),
        name="conv",
    )(pos, *blocks, *tables, parts, *joined))


def run_conv_plain(blocks, tables, filt, repeats, orient):
    sources, shard_rows, rows, width = blocks.shape
    n_one, n_two = tables[4].shape
    times = sources * shard_rows
    half = rows // 2
    filters = filt[0].shape[0]
    filt_spec = pl.BlockSpec(
        (1, n_one, n_two), lambda place: (jnp.minimum(place // repeats, filters - 1), 0, 0)
    )
    moved = 4 * blocks.size
    signal = blocks.reshape(times, 2, half, width).transpose(2, 1, 0, 3)
    signal = signal.reshape(half, 2 * times, width)
    channel_spec = pl.BlockSpec((1, 2 * times, width), lambda place: (place, 0, 0))
    result = pl.pallas_call(
        functools.partial(conv_plain_kernel, orient=orient),
        grid=(half,),
        in_specs=[channel_spec] + [whole(table.shape) for table in tables] + [filt_spec] * 2,
        out_specs=channel_spec,
        out_shape=jax.ShapeDtypeStruct(signal.shape, BF),
        scratch_shapes=[pltpu.VMEM((2 * n_one, n_two), BF)],
        compiler_params=params(),
        cost_estimate=conv_cost(half, n_one, n_two, moved),
        name="conv_plain",
    )(signal, *tables, *filt)
    result = result.reshape(half, 2, times, width).transpose(2, 1, 0, 3)
    return result.reshape(blocks.shape)


def store_sum(pos_ref, total, sum_ref, turn_ref, peers, blocks, chunks, rows):
    pos = pos_ref[0]
    kinds = total.shape[0] // (len(blocks) * chunks * rows)
    spot = 0
    if len(blocks) < peers:
        turn_ref[...] = jnp.zeros_like(turn_ref)
    for kind in range(kinds):
        for block in blocks:
            for chunk in range(chunks):
                start = ((kind * chunks + chunk) * peers + (pos ^ block)) * rows
                span = pl.ds(pl.multiple_of(start, rows), rows)
                turn_ref[span, :] = total[spot : spot + rows]
                spot += rows
    sum_ref[...] = turn_ref[...].T


def smooth_kernel(pos_ref, tok_ref, cot_ref, w_ref, pick_ref, *rest):
    parts, (gated_ref, sum_ref, held_ref, wt_ref, total_ref, turn_ref) = rest[:-6], rest[-6:]
    chunks, steps, rows, width = parts[0].shape
    peers = len(parts)
    chan = pick_ref.shape[1]

    @pl.when(pl.program_id(0) == 0)
    def _():
        gather_rows(pos_ref, pick_ref, held_ref, peers, range(peers), rows)
        wt_ref[...] = dot_nt(held_ref[...], w_ref[:, :chan]).astype(BF)
        total_ref[...] = jnp.zeros_like(total_ref)

    total = total_ref[...]
    for step in range(steps):
        span = slice(step * width, (step + 1) * width)
        tokens = tok_ref[span, :]
        gate = rounded(dot_nt(wt_ref[...], tokens))
        cot = dot_nt(held_ref[...], cot_ref[span, :])
        smooth = load_blocks(parts, step)
        gated_ref[span, :] = dot_tn((gate * smooth).astype(BF), held_ref[...]).astype(BF)
        total = total + dot_nn((cot * smooth).astype(BF), tokens)
    total_ref[...] = total

    @pl.when(pl.program_id(0) == pl.num_programs(0) - 1)
    def _():
        store_sum(pos_ref, total, sum_ref, turn_ref, peers, range(peers), chunks, rows)


def back_kernel(pos_ref, tok_ref, w_ref, pick_ref, *rest, peers, blocks):
    parts, rest = rest[: len(blocks)], rest[len(blocks) :]
    earlier, (sum_ref, held_ref, wt_ref, total_ref, turn_ref) = rest[:-5], rest[-5:]
    chunks, steps, rows, width = parts[0].shape
    count = len(blocks) * chunks * rows

    @pl.when(pl.program_id(0) == 0)
    def _():
        gather_rows(pos_ref, pick_ref, held_ref, peers, blocks, rows)
        key_value_weights(w_ref, held_ref, wt_ref)
        total_ref[...] = jnp.zeros_like(total_ref)

    total = total_ref[...]
    for step in range(steps):
        tokens = tok_ref[step * width : (step + 1) * width, :]
        feats = rounded(dot_nt(wt_ref[...], tokens))
        mixed = load_blocks(parts, step)
        grads = jnp.concatenate(
            [(mixed * feats[count:]).astype(BF), (mixed * feats[:count]).astype(BF)], axis=0
        )
        total = total + dot_nn(grads, tokens)
    total_ref[...] = total

    @pl.when(pl.program_id(0) == pl.num_programs(0) - 1)
    def _():
        store_sum(pos_ref, total, sum_ref, turn_ref, peers, blocks, chunks, rows)
        for ref in earlier:
            sum_ref[...] += ref[...]


def halves(peers):
    order = [block for block in range(2, peers, 2)] + [block for block in range(3, peers, 2)]
    return tuple(order[: peers // 2 - 1]), tuple(order[peers // 2 - 1 :] + [1, 0])


def send(blocks, group):
    arrived = list(blocks)
    peers = len(blocks)
    for block in group:
        if block:
            pairs = [(device, device ^ block) for device in range(peers)]
            arrived[block] = lax.ppermute(blocks[block], "ctx", pairs)
    return arrived


def exchange(blocks):
    return lax.all_to_all(blocks, "ctx", split_axis=0, concat_axis=0, tiled=True)


def own_filters(filter_real, filter_imag, ctx_count, group_count, group_pos):
    rows, n_two, filters = filter_real.shape
    quarter = rows // group_count
    own = lax.dynamic_slice_in_dim(
        jnp.stack([filter_real, filter_imag]), group_pos * quarter, quarter, 1
    )
    own = own.astype(BF).transpose(3, 0, 1, 2)
    if ctx_count > filters:
        own = jnp.repeat(own, ctx_count // filters, axis=0)
    return own.reshape(ctx_count, own.shape[0] // ctx_count, 2, quarter, n_two)


def gather_filters(own):
    return lax.all_gather(exchange(own), "dp", axis=0, tiled=False)


def after(first, value):
    return lax.optimization_barrier((value, first))


def reduce_groups(value):
    count = lax.axis_size("dp")
    pos = lax.axis_index("dp")
    split = value.reshape(count, value.shape[0] // count, value.shape[1])
    total = lax.dynamic_index_in_dim(split, pos, 0, keepdims=False)
    for step in range(1, count):
        pairs = [(device, (device + step) % count) for device in range(count)]
        sent = lax.dynamic_index_in_dim(split, (pos + step) % count, 0, keepdims=False)
        total = total + lax.ppermute(sent, "dp", pairs)
    return total


def reduce_tokens(value):
    count = lax.axis_size("ctx")
    step = 1
    while step < count:
        pairs = [(device, device ^ step) for device in range(count)]
        value = value + lax.ppermute(value, "ctx", pairs)
        step *= 2
    return value


def with_kernels(arrays, tables, pick, chunks, repeats, group_pos):
    tokens, cotangent, w_in, filter_real, filter_imag = arrays
    peers = lax.axis_size("ctx")
    tok_rows, chan = tokens.shape
    width = tables[4].shape[1]
    shard_rows = tok_rows // width
    rows = chan // (peers * chunks)
    count = peers * rows
    me = lax.axis_index("ctx").astype(jnp.int32)
    pos = me.reshape(1)
    steps = math.gcd(shard_rows, 4)
    grid = (shard_rows // steps,)
    tok_spec = pl.BlockSpec((steps * width, chan), lambda i: (i, 0))
    part_spec = pl.BlockSpec((chunks, steps, rows, width), lambda i: (0, i, 0, 0))
    chunk_spec = pl.BlockSpec((1, steps, rows, width), lambda i: (0, i, 0, 0))
    part_out = jax.ShapeDtypeStruct((chunks, shard_rows, rows, width), BF)
    w_spec, pick_spec = whole(w_in.shape), whole(pick.shape)
    macs = tok_rows * chan * chan

    def held(count, kind=BF):
        return pltpu.VMEM((count, chan), kind)

    def cost(times, moved):
        return pl.CostEstimate(
            flops=int(2 * macs * times), bytes_accessed=int(moved * 2 * tok_rows * chan),
            transcendentals=0,
        )

    def conv(blocks, chunk, orient, last, joined):
        return run_conv(blocks, tables, parts, chunk, repeats, orient, last, joined)

    def shaped(blocks, shape):
        return [block.reshape(shape) for block in blocks]

    early, late = halves(peers)
    first_group, second_group = early + late[:1], late[1:]
    flat = (chunks, shard_rows * rows, width)

    mixed = [None] * peers
    last = pos
    for group in (first_group, second_group):
        some = len(group) * chunks * rows
        outs = pl.pallas_call(
            functools.partial(mixed_kernel, peers=peers, blocks=group),
            grid=grid,
            in_specs=[POS_SPEC, tok_spec, w_spec, pick_spec],
            out_specs=[part_spec] * len(group),
            out_shape=[part_out] * len(group),
            scratch_shapes=[held(some), held(2 * some)],
            compiler_params=params(),
            cost_estimate=cost(1, 1.5),
            name="mixed",
        )(last, tokens, w_in, pick)
        last, outs = after(list(outs), pos)
        for block, out in zip(group, outs):
            mixed[block] = out
    own = own_filters(filter_real, filter_imag, peers, lax.axis_size("dp"), group_pos)
    own, mixed[0] = after(mixed[0], own)
    mine = exchange(own)
    arrived = send(send(mixed, first_group), second_group)
    (last, mine), held_back = after([arrived[block] for block in early], (last, mine))
    for block, value in zip(early, held_back):
        arrived[block] = value
    grads = list(pl.pallas_call(
        functools.partial(grad_kernel, peers=peers),
        grid=grid,
        in_specs=[POS_SPEC, tok_spec, tok_spec, w_spec, pick_spec],
        out_specs=[part_spec] * peers,
        out_shape=[part_out] * peers,
        scratch_shapes=[held(chan), held(chan)],
        compiler_params=params(),
        cost_estimate=cost(2, 3),
        name="grad_smooth",
    )(last, tokens, cotangent, w_in, pick))
    parts = lax.all_gather(mine, "dp", axis=0, tiled=False)

    arrived = shaped(arrived, flat)
    grads = shaped(grads, flat)
    joined = conv(arrived, 0, 1.0, pos, [])
    grads = send(grads, early)
    (last, grads), joined = after(joined, (pos, grads))
    joined = conv(arrived, 1, 1.0, last, joined)
    grads = send(grads, late)
    last, joined = after(joined, pos)
    back = conv(grads, 0, -1.0, last, [])
    smooth = send(joined, early)
    (last, smooth), back = after(back, (pos, smooth))
    back = conv(grads, 1, -1.0, last, back)
    smooth = send(smooth, late)
    last, back = after(back, pos)
    back = send(back, early)

    gated, gate_sum = pl.pallas_call(
        smooth_kernel,
        grid=grid,
        in_specs=[POS_SPEC, tok_spec, tok_spec, w_spec, pick_spec] + [part_spec] * peers,
        out_specs=[tok_spec, pl.BlockSpec((chan, chan), lambda i: (0, 0))],
        out_shape=[
            jax.ShapeDtypeStruct((tok_rows, chan), BF), jax.ShapeDtypeStruct((chan, chan), F32)
        ],
        scratch_shapes=[held(chan), held(chan), held(chan, F32), held(chan, F32)],
        compiler_params=params(),
        cost_estimate=cost(4, 4),
        name="smooth",
    )(last, tokens, cotangent, w_in, pick, *shaped(smooth, part_out.shape))
    (last, back), gate_sum = after(gate_sum, (pos, back))
    back = send(back, late)
    sum_shape = (chan, 2 * chan)
    back_sum = []
    for group in (early, late):
        some = len(group) * chunks * rows
        blocks = shaped([back[block] for block in group], part_out.shape)
        back_sum = [pl.pallas_call(
            functools.partial(back_kernel, peers=peers, blocks=group),
            grid=grid,
            in_specs=[POS_SPEC, tok_spec, w_spec, pick_spec] + [part_spec] * len(group)
            + [whole(sum_shape)] * len(back_sum),
            out_specs=pl.BlockSpec(sum_shape, lambda i: (0, 0)),
            out_shape=jax.ShapeDtypeStruct(sum_shape, F32),
            scratch_shapes=[
                held(some), held(2 * some), held(2 * some, F32), held(2 * chan, F32)
            ],
            compiler_params=params(),
            cost_estimate=cost(2, 2),
            name="back",
        )(last, tokens, w_in, pick, *blocks, *back_sum)]
        if group == early:
            gate_sum, back_sum = after(back_sum, gate_sum)
            gate_sum = reduce_tokens(reduce_groups(gate_sum))
            last, gate_sum = after(gate_sum, pos)
    return gated, gate_sum, reduce_tokens(reduce_groups(back_sum[0]))


def without_kernels(arrays, tables, pick, rows, repeats, group_pos):
    tokens, cotangent, w_in, filter_real, filter_imag = arrays
    peers = lax.axis_size("ctx")
    tok_rows, chan = tokens.shape
    width = tables[4].shape[1]
    shard_rows = tok_rows // width
    wt = [
        dot_nt(pick, w_in[:, part * chan : (part + 1) * chan]).astype(BF) for part in range(3)
    ]
    gate, key, value = [dot_nt(block, tokens).astype(BF).astype(F32) for block in wt]
    cot = dot_nt(pick, cotangent)
    own = own_filters(filter_real, filter_imag, peers, lax.axis_size("dp"), group_pos)
    parts = gather_filters(own)
    groups, _, each, _, quarter, _ = parts.shape
    filt = parts.transpose(3, 2, 1, 0, 4, 5).reshape(2, each, peers * groups * quarter, width)

    def convolved(array, orient):
        array = array.astype(BF).reshape(peers, rows, shard_rows, width).transpose(0, 2, 1, 3)
        result = run_conv_plain(exchange(array), tables, (filt[0], filt[1]), repeats, orient)
        result = exchange(result).transpose(0, 2, 1, 3)
        return result.reshape(chan, tok_rows).astype(F32)

    smooth = convolved(key * value, 1.0)
    back = convolved(gate * cot, -1.0)
    gated = dot_tn((gate * smooth).astype(BF), pick).astype(BF)
    terms = [cot * smooth, back * value, back * key]
    sums = [dot_nn(term.astype(BF), tokens).T for term in terms]
    summed = reduce_tokens(reduce_groups(jnp.concatenate(sums, axis=1)))
    return gated, summed[:, :chan], summed[:, chan:]


def per_device(inputs, grad_out, w_in, filter_real, filter_imag):
    ctx_count = lax.axis_size("ctx")
    group_count = lax.axis_size("dp")
    tokens = inputs[0]
    cotangent = grad_out[0]
    tok_rows, chan_total = tokens.shape
    chan_half = chan_total // 2
    n_one = filter_real.shape[0] * ctx_count
    n_two = filter_real.shape[1]
    filters = filter_real.shape[2]
    repeats = chan_half // filters
    seq_len = n_one * n_two // 2
    shard_rows = tok_rows // n_two
    per_device_chan = chan_half // ctx_count
    quarter = filter_real.shape[0] // group_count
    use_kernels = (
        per_device_chan % 16 == 0 and quarter % 16 == 0 and repeats % (per_device_chan // 2) == 0
        and ctx_count & (ctx_count - 1) == 0
    )
    chunks = 2 if use_kernels else 1
    rows = 2 * (per_device_chan // chunks)

    tables = tuple(jnp.asarray(table) for table in transform_tables(n_one, n_two))
    order = channel_order(chan_half, filters, ctx_count, chunks)
    pick_np = np.zeros((chan_total, chan_total), np.float32)
    pick_np[np.arange(chan_total), order] = 1.0
    pick = jnp.asarray(pick_np.astype(ml_dtypes.bfloat16))
    group_pos = lax.axis_index("dp")
    arrays = (tokens, cotangent, w_in, filter_real, filter_imag)
    if use_kernels:
        gated, gate_sum, back_sum = with_kernels(
            arrays, tables, pick, chunks, repeats, group_pos
        )
    else:
        gated, gate_sum, back_sum = without_kernels(
            arrays, tables, pick, rows, repeats, group_pos
        )

    scale = 1.0 / math.sqrt(inputs.shape[0] * group_count * seq_len)

    summed = jnp.concatenate([gate_sum, back_sum], axis=1)
    ordered = jnp.dot(
        summed.reshape(-1, chan_total), pick.astype(F32), precision=lax.Precision.HIGHEST
    )
    summed = ordered.reshape(summed.shape)
    return (gated[None], summed * scale)


def solution(mesh):
    placed = (
        P("dp", "ctx", None),
        P("dp", "ctx", None),
        P(),
        P("ctx", None, None),
        P("ctx", None, None),
    )
    return jax.shard_map(
        per_device,
        mesh=mesh,
        in_specs=placed,
        out_specs=(P("dp", "ctx", None), P("dp", None)),
        check_vma=False,
    )
```

```python
import functools
import math

import jax
import jax.numpy as jnp
import ml_dtypes
import numpy as np
from jax import lax
from jax.experimental import pallas as pl
from jax.experimental.pallas import tpu as pltpu
from jax.sharding import PartitionSpec as P

BF = jnp.bfloat16
F32 = jnp.float32
VMEM_BYTES = 60 * 1024 * 1024
POS_SPEC = pl.BlockSpec(memory_space=pltpu.SMEM)


def dot_nn(left, right):
    return lax.dot_general(left, right, (((1,), (0,)), ((), ())), preferred_element_type=F32)


def dot_nt(left, right):
    return lax.dot_general(left, right, (((1,), (1,)), ((), ())), preferred_element_type=F32)


def dot_tn(left, right):
    return lax.dot_general(left, right, (((0,), (0,)), ((), ())), preferred_element_type=F32)


def rounded(value):
    return value.astype(BF).astype(F32)


def transform_tables(n_one, n_two):
    def table(rows, cols, period):
        angle = (np.arange(rows)[:, None] * np.arange(cols)[None, :] % period) * (
            2.0 * math.pi / period
        )
        factor = 1.0 / math.sqrt(period)
        return (
            (np.cos(angle) * factor).astype(np.float32).astype(ml_dtypes.bfloat16),
            (np.sin(angle) * factor).astype(np.float32).astype(ml_dtypes.bfloat16),
        )

    cos_one, sin_one = table(n_one, n_one // 2, n_one)
    cos_two, sin_two = table(n_two, n_two, n_two)
    period = n_one * n_two
    angle = (np.arange(n_one)[:, None] * np.arange(n_two)[None, :] % period) * (
        2.0 * math.pi / period
    )
    first = np.block([[cos_one, sin_one], [-sin_one, cos_one]])
    second = np.block([[cos_two, -sin_two], [sin_two, cos_two]])
    third = np.block([[cos_two, sin_two], [-sin_two, cos_two]])
    fourth = np.block([[cos_one.T, -sin_one.T], [sin_one.T, cos_one.T]])
    return (
        first,
        second,
        third,
        fourth,
        np.cos(angle).astype(np.float32),
        np.sin(angle).astype(np.float32),
    )


def channel_order(chan_half, filters, ctx_count, chunks):
    repeats = chan_half // filters
    per_device = chan_half // ctx_count
    per_chunk = per_device // chunks
    order = []
    for chunk in range(chunks):
        for device in range(ctx_count):
            for part in range(2):
                for place in range(per_chunk):
                    index = device * per_device + chunk * per_chunk + place
                    group, repeat = divmod(index, repeats)
                    order.append(part * chan_half + repeat * filters + group)
    return np.array(order)


def gather_rows(pos_ref, pick_ref, held_ref, peers, blocks, rows):
    pos = pos_ref[0]
    chunks = pick_ref.shape[0] // (peers * rows)
    spot = 0
    for block in blocks:
        for chunk in range(chunks):
            start = pl.multiple_of((chunk * peers + (pos ^ block)) * rows, rows)
            held_ref[spot : spot + rows, :] = pick_ref[pl.ds(start, rows), :]
            spot += rows


def key_value_weights(w_ref, held_ref, wt_ref):
    count, chan = held_ref.shape
    for part in range(2):
        block = w_ref[:, (1 + part) * chan : (2 + part) * chan]
        wt_ref[part * count : (part + 1) * count, :] = dot_nt(held_ref[...], block).astype(BF)


def store_blocks(value, outs, step):
    chunks, _, rows, _ = outs[0].shape
    spot = 0
    for out in outs:
        for chunk in range(chunks):
            out[chunk, step] = value[spot : spot + rows]
            spot += rows


def load_blocks(parts, step):
    chunks = parts[0].shape[0]
    return jnp.concatenate(
        [part[chunk, step] for part in parts for chunk in range(chunks)], axis=0
    ).astype(F32)


def mixed_kernel(pos_ref, tok_ref, w_ref, pick_ref, *rest, peers, blocks):
    outs, (held_ref, wt_ref) = rest[:-2], rest[-2:]
    _, steps, rows, width = outs[0].shape
    count = held_ref.shape[0]

    @pl.when(pl.program_id(0) == 0)
    def _():
        gather_rows(pos_ref, pick_ref, held_ref, peers, blocks, rows)
        key_value_weights(w_ref, held_ref, wt_ref)

    for step in range(steps):
        feats = rounded(dot_nt(wt_ref[...], tok_ref[step * width : (step + 1) * width, :]))
        store_blocks((feats[:count] * feats[count:]).astype(BF), outs, step)


def grad_kernel(pos_ref, tok_ref, cot_ref, w_ref, pick_ref, *rest, peers):
    outs, (held_ref, wt_ref) = rest[:-2], rest[-2:]
    _, steps, rows, width = outs[0].shape
    chan = pick_ref.shape[1]

    @pl.when(pl.program_id(0) == 0)
    def _():
        gather_rows(pos_ref, pick_ref, held_ref, peers, range(peers), rows)
        wt_ref[...] = dot_nt(held_ref[...], w_ref[:, :chan]).astype(BF)

    for step in range(steps):
        span = slice(step * width, (step + 1) * width)
        gate = rounded(dot_nt(wt_ref[...], tok_ref[span, :]))
        cot = dot_nt(held_ref[...], cot_ref[span, :])
        store_blocks((gate * cot).astype(BF), outs, step)


def convolve(signal, refs, filt_real, filt_imag, orient, hold_ref):
    first_ref, second_ref, third_ref, fourth_ref, cos_ref, sin_ref = refs
    n_one, n_two = cos_ref.shape
    cos, sin = cos_ref[...], sin_ref[...]
    partial = dot_nn(first_ref[...], signal)
    real, imag = partial[:n_one], partial[n_one:]
    turned = jnp.concatenate(
        [(real * cos + imag * sin).astype(BF), (imag * cos - real * sin).astype(BF)], axis=1
    )
    spec = dot_nn(turned, second_ref[...])
    real, imag = spec[:, :n_two], spec[:, n_two:]
    f_real = filt_real.astype(F32)
    f_imag = filt_imag.astype(F32) * orient
    product = jnp.concatenate(
        [
            (real * f_real - imag * f_imag).astype(BF),
            (real * f_imag + imag * f_real).astype(BF),
        ],
        axis=1,
    )
    back = dot_nn(product, third_ref[...])
    real, imag = back[:, :n_two], back[:, n_two:]
    hold_ref[:n_one, :] = (real * cos - imag * sin).astype(BF)
    hold_ref[n_one:, :] = (imag * cos + real * sin).astype(BF)
    return dot_nn(fourth_ref[...], hold_ref[...])


def conv_kernel(pos_ref, *args, peers, rows, orient):
    ins, rest = args[:peers], args[peers:]
    tables, rest = rest[:6], rest[6:]
    parts_ref, rest = rest[0], rest[1:]
    outs, (in_ref, res_ref, hold_ref, filt_ref) = rest[-4 - peers : -4], rest[-4:]
    lanes = 128
    _, size, width = ins[0].shape
    times = peers * size // rows
    half = rows // 2
    place = pl.program_id(0)
    pos = pos_ref[0]
    piece = math.gcd(size, 256)

    @pl.when(place == 0)
    def _():
        groups, _, _, _, quarter, _ = parts_ref.shape
        for block in range(peers):
            base = (pos ^ block) * size
            for group in range(groups):
                start = (block * groups + group) * quarter
                span = slice(start, start + quarter)
                for part in range(2):
                    filt_ref[part, span, :] = parts_ref[group, block, 0, part]

            @pl.loop(0, size // piece)
            def _(index):
                wide = ins[block][0, pl.ds(pl.multiple_of(index * piece, piece), piece), :]
                wide = wide.astype(F32)
                span = pl.ds(pl.multiple_of(base + index * piece, piece), piece)
                for lane in range(width // lanes):
                    in_ref[lane, span, :] = wide[:, lane * lanes : (lane + 1) * lanes]

    parts = []
    for part in range(2):
        columns = [
            in_ref[lane, pl.ds(place + part * half, times, stride=rows), :].astype(BF)
            for lane in range(width // lanes)
        ]
        parts.append(jnp.concatenate(columns, axis=1))
    signal = jnp.concatenate(parts, axis=0)
    result = convolve(
        signal,
        tables,
        filt_ref[0],
        filt_ref[1],
        orient,
        hold_ref,
    )
    for part in range(2):
        for lane in range(width // lanes):
            res_ref[lane, pl.ds(place + part * half, times, stride=rows), :] = result[
                part * times : (part + 1) * times, lane * lanes : (lane + 1) * lanes
            ]

    @pl.when(place == pl.num_programs(0) - 1)
    def _():
        for block in range(peers):
            base = (pos ^ block) * size

            @pl.loop(0, size // piece)
            def _(index):
                span = pl.ds(pl.multiple_of(base + index * piece, piece), piece)
                outs[block][0, pl.ds(pl.multiple_of(index * piece, piece), piece), :] = (
                    jnp.concatenate(
                        [res_ref[lane, span, :] for lane in range(width // lanes)], axis=1
                    ).astype(BF)
                )


def conv_plain_kernel(x_ref, first, second, third, fourth, cos, sin, fr_ref, fi_ref, out_ref,
                      hold_ref, *, orient):
    out_ref[0] = convolve(
        x_ref[0],
        (first, second, third, fourth, cos, sin),
        fr_ref[0],
        fi_ref[0],
        orient,
        hold_ref,
    ).astype(BF)


def whole(shape):
    zeros = (0,) * len(shape)
    return pl.BlockSpec(shape, lambda *_: zeros, pipeline_mode=pl.Buffered(1))


def params():
    return pltpu.CompilerParams(
        dimension_semantics=("arbitrary",), vmem_limit_bytes=VMEM_BYTES
    )


def conv_cost(count, n_one, n_two, moved):
    macs = count * 2 * (n_one * n_one * n_two + 2 * n_one * n_two * n_two)
    return pl.CostEstimate(flops=2 * macs, bytes_accessed=moved, transcendentals=0)


def run_conv(blocks, tables, parts, chunk, repeats, orient, pos, joined):
    peers = len(blocks)
    chunks, size, width = blocks[0].shape
    n_one, n_two = tables[4].shape
    rows = size * peers // (n_one // 2)
    half = rows // 2
    table_specs = [whole(table.shape) for table in tables]
    block_spec = pl.BlockSpec(
        (1, size, width), lambda place: (chunk, 0, 0), pipeline_mode=pl.Buffered(1)
    )
    parts_shape = parts.shape[:2] + (1,) + parts.shape[3:]
    place_of = (0, 0, chunk * half // repeats, 0, 0, 0)
    parts_spec = pl.BlockSpec(
        parts_shape, lambda place: place_of, pipeline_mode=pl.Buffered(1)
    )
    moved = 4 * peers * size * width
    moved += sum(table.size * table.dtype.itemsize for table in tables)
    slots = pltpu.VMEM((width // 128, peers * size, 128), F32)
    first = 1 + peers + len(tables) + 1
    out_spec = pl.BlockSpec((1, size, width), lambda place: (chunk, 0, 0))
    return list(pl.pallas_call(
        functools.partial(conv_kernel, peers=peers, rows=rows, orient=orient),
        grid=(half,),
        in_specs=[POS_SPEC] + [block_spec] * peers + table_specs + [parts_spec]
        + [pl.BlockSpec(memory_space=pl.ANY)] * len(joined),
        out_specs=[out_spec] * peers,
        out_shape=[jax.ShapeDtypeStruct((chunks, size, width), BF)] * peers,
        input_output_aliases={first + index: index for index in range(len(joined))},
        scratch_shapes=[
            slots, slots, pltpu.VMEM((2 * n_one, n_two), BF), pltpu.VMEM((2, n_one, n_two), BF)
        ],
        compiler_params=params(),
        cost_estimate=conv_cost(half, n_one, n_two, moved),
        name="conv",
    )(pos, *blocks, *tables, parts, *joined))


def run_conv_plain(blocks, tables, filt, repeats, orient):
    sources, shard_rows, rows, width = blocks.shape
    n_one, n_two = tables[4].shape
    times = sources * shard_rows
    half = rows // 2
    filters = filt[0].shape[0]
    filt_spec = pl.BlockSpec(
        (1, n_one, n_two), lambda place: (jnp.minimum(place // repeats, filters - 1), 0, 0)
    )
    moved = 4 * blocks.size
    signal = blocks.reshape(times, 2, half, width).transpose(2, 1, 0, 3)
    signal = signal.reshape(half, 2 * times, width)
    channel_spec = pl.BlockSpec((1, 2 * times, width), lambda place: (place, 0, 0))
    result = pl.pallas_call(
        functools.partial(conv_plain_kernel, orient=orient),
        grid=(half,),
        in_specs=[channel_spec] + [whole(table.shape) for table in tables] + [filt_spec] * 2,
        out_specs=channel_spec,
        out_shape=jax.ShapeDtypeStruct(signal.shape, BF),
        scratch_shapes=[pltpu.VMEM((2 * n_one, n_two), BF)],
        compiler_params=params(),
        cost_estimate=conv_cost(half, n_one, n_two, moved),
        name="conv_plain",
    )(signal, *tables, *filt)
    result = result.reshape(half, 2, times, width).transpose(2, 1, 0, 3)
    return result.reshape(blocks.shape)


def store_sum(pos_ref, total, outs, turn_ref, flat_ref, peers, blocks, chunks, rows, earlier):
    pos = pos_ref[0]
    kinds = total.shape[0] // (len(blocks) * chunks * rows)
    spot = 0
    if len(blocks) < peers:
        turn_ref[...] = jnp.zeros_like(turn_ref)
    for kind in range(kinds):
        for block in blocks:
            for chunk in range(chunks):
                start = ((kind * chunks + chunk) * peers + (pos ^ block)) * rows
                span = pl.ds(pl.multiple_of(start, rows), rows)
                turn_ref[span, :] = total[spot : spot + rows]
                spot += rows
    summed = turn_ref[...].T
    for ref in earlier:
        summed = summed + ref[...]
    if len(outs) == 1:
        outs[0][...] = summed
        return
    flat_ref[...] = summed
    keep_ref, sent_ref = outs
    groups, size, _ = keep_ref.shape
    core = pos % 2
    for group in range(groups):
        base = lax.rem(pos_ref[1] + group, groups) * (2 * size)
        keep_ref[group] = flat_ref[pl.ds(pl.multiple_of(base + core * size, size), size), :]
        sent_ref[group] = flat_ref[pl.ds(pl.multiple_of(base + (1 - core) * size, size), size), :]


def smooth_kernel(pos_ref, tok_ref, cot_ref, w_ref, pick_ref, *rest):
    parts, (gated_ref, *outs) = rest[:-7], rest[-7:-4]
    held_ref, wt_ref, total_ref, turn_ref = rest[-4:]
    chunks, steps, rows, width = parts[0].shape
    peers = len(parts)
    chan = pick_ref.shape[1]

    @pl.when(pl.program_id(0) == 0)
    def _():
        gather_rows(pos_ref, pick_ref, held_ref, peers, range(peers), rows)
        wt_ref[...] = dot_nt(held_ref[...], w_ref[:, :chan]).astype(BF)
        total_ref[...] = jnp.zeros_like(total_ref)

    total = total_ref[...]
    for step in range(steps):
        span = slice(step * width, (step + 1) * width)
        tokens = tok_ref[span, :]
        gate = rounded(dot_nt(wt_ref[...], tokens))
        cot = dot_nt(held_ref[...], cot_ref[span, :])
        smooth = load_blocks(parts, step)
        gated_ref[span, :] = dot_tn((gate * smooth).astype(BF), held_ref[...]).astype(BF)
        total = total + dot_nn((cot * smooth).astype(BF), tokens)
    total_ref[...] = total

    @pl.when(pl.program_id(0) == pl.num_programs(0) - 1)
    def _():
        store_sum(
            pos_ref, total, outs, turn_ref, total_ref, peers, range(peers), chunks, rows, []
        )


def back_terms(parts, feats, tokens, step):
    count = feats.shape[0] // 2
    mixed = load_blocks(parts, step)
    grads = [mixed * feats[count:], mixed * feats[:count]]
    return dot_nn(jnp.concatenate([grad.astype(BF) for grad in grads], axis=0), tokens)


def back_first_kernel(pos_ref, tok_ref, w_ref, pick_ref, *rest, peers, blocks, others):
    parts, (sum_ref, feat_ref) = rest[: len(blocks)], rest[len(blocks) : -5]
    held_ref, later_ref, wt_ref, total_ref, turn_ref = rest[-5:]
    chunks, steps, rows, width = parts[0].shape
    count = 2 * held_ref.shape[0]

    @pl.when(pl.program_id(0) == 0)
    def _():
        gather_rows(pos_ref, pick_ref, held_ref, peers, blocks, rows)
        gather_rows(pos_ref, pick_ref, later_ref, peers, others, rows)
        key_value_weights(w_ref, held_ref, wt_ref.at[:count])
        key_value_weights(w_ref, later_ref, wt_ref.at[count:])
        total_ref[...] = jnp.zeros_like(total_ref)

    total = total_ref[...]
    for step in range(steps):
        span = slice(step * width, (step + 1) * width)
        tokens = tok_ref[span, :]
        feats = dot_nt(wt_ref[...], tokens).astype(BF)
        feat_ref[:, span] = feats[count:]
        total = total + back_terms(parts, feats[:count].astype(F32), tokens, step)
    total_ref[...] = total

    @pl.when(pl.program_id(0) == pl.num_programs(0) - 1)
    def _():
        store_sum(
            pos_ref, total, [sum_ref], turn_ref, None, peers, blocks, chunks, rows, []
        )


def back_last_kernel(pos_ref, tok_ref, feat_ref, earlier_ref, *rest, peers, blocks):
    parts, outs = rest[: len(blocks)], rest[len(blocks) : -3]
    total_ref, turn_ref, flat_ref = rest[-3:]
    chunks, steps, rows, width = parts[0].shape

    @pl.when(pl.program_id(0) == 0)
    def _():
        total_ref[...] = jnp.zeros_like(total_ref)

    total = total_ref[...]
    for step in range(steps):
        span = slice(step * width, (step + 1) * width)
        feats = feat_ref[:, span].astype(F32)
        total = total + back_terms(parts, feats, tok_ref[span, :], step)
    total_ref[...] = total

    @pl.when(pl.program_id(0) == pl.num_programs(0) - 1)
    def _():
        store_sum(
            pos_ref, total, outs, turn_ref, flat_ref, peers, blocks, chunks, rows, [earlier_ref]
        )


def halves(peers):
    order = [block for block in range(2, peers, 2)] + [block for block in range(3, peers, 2)]
    return tuple(order[: peers // 2 - 1]), tuple(order[peers // 2 - 1 :] + [1, 0])


def send(blocks, group):
    arrived = list(blocks)
    peers = len(blocks)
    for block in group:
        if block:
            pairs = [(device, device ^ block) for device in range(peers)]
            arrived[block] = lax.ppermute(blocks[block], "ctx", pairs)
    return arrived


def exchange(blocks):
    return lax.all_to_all(blocks, "ctx", split_axis=0, concat_axis=0, tiled=True)


def own_filters(filter_real, filter_imag, ctx_count, group_count, group_pos):
    rows, n_two, filters = filter_real.shape
    quarter = rows // group_count
    own = lax.dynamic_slice_in_dim(
        jnp.stack([filter_real, filter_imag]), group_pos * quarter, quarter, 1
    )
    own = own.astype(BF).transpose(3, 0, 1, 2)
    if ctx_count > filters:
        own = jnp.repeat(own, ctx_count // filters, axis=0)
    return own.reshape(ctx_count, own.shape[0] // ctx_count, 2, quarter, n_two)


def gather_filters(own):
    return lax.all_gather(exchange(own), "dp", axis=0, tiled=False)


def after(first, value):
    return lax.optimization_barrier((value, first))


def reduce_groups(value):
    count = lax.axis_size("dp")
    pos = lax.axis_index("dp")
    split = value.reshape(count, value.shape[0] // count, value.shape[1])
    total = lax.dynamic_index_in_dim(split, pos, 0, keepdims=False)
    for step in range(1, count):
        pairs = [(device, (device + step) % count) for device in range(count)]
        sent = lax.dynamic_index_in_dim(split, (pos + step) % count, 0, keepdims=False)
        total = total + lax.ppermute(sent, "dp", pairs)
    return total


def reduce_tokens(value):
    count = lax.axis_size("ctx")
    step = 1
    while step < count:
        pairs = [(device, device ^ step) for device in range(count)]
        value = value + lax.ppermute(value, "ctx", pairs)
        step *= 2
    return value


def swap(value, step):
    pairs = [(device, device ^ step) for device in range(lax.axis_size("ctx"))]
    return lax.ppermute(value, "ctx", pairs)


def reduce_kept(keep, sent):
    keep = keep + swap(sent, 1)
    groups = lax.axis_size("dp")
    total = keep[0]
    for step in range(1, groups):
        pairs = [(device, (device + step) % groups) for device in range(groups)]
        total = total + lax.ppermute(keep[step], "dp", pairs)
    return total


def reduce_chips(total):
    step = 2
    while step < lax.axis_size("ctx"):
        total = total + swap(total, step)
        step *= 2
    other = swap(total, 1)
    upper = lax.axis_index("ctx") % 2 != 0
    return jnp.concatenate([jnp.where(upper, other, total), jnp.where(upper, total, other)])


def with_kernels(arrays, tables, pick, chunks, repeats, group_pos):
    tokens, cotangent, w_in, filter_real, filter_imag = arrays
    peers = lax.axis_size("ctx")
    tok_rows, chan = tokens.shape
    width = tables[4].shape[1]
    shard_rows = tok_rows // width
    rows = chan // (peers * chunks)
    count = peers * rows
    me = lax.axis_index("ctx").astype(jnp.int32)
    pos = jnp.stack([me, group_pos.astype(jnp.int32)])
    groups = lax.axis_size("dp")

    def specs(most):
        steps = math.gcd(shard_rows, most)
        return (
            (shard_rows // steps,),
            pl.BlockSpec((steps * width, chan), lambda i: (i, 0)),
            pl.BlockSpec((chunks, steps, rows, width), lambda i: (0, i, 0, 0)),
        )

    part_out = jax.ShapeDtypeStruct((chunks, shard_rows, rows, width), BF)
    w_spec, pick_spec = whole(w_in.shape), whole(pick.shape)
    macs = tok_rows * chan * chan

    def held(count, kind=BF):
        return pltpu.VMEM((count, chan), kind)

    def cost(times, moved):
        return pl.CostEstimate(
            flops=int(2 * macs * times), bytes_accessed=int(moved * 2 * tok_rows * chan),
            transcendentals=0,
        )

    def conv(blocks, chunk, orient, last, joined):
        return run_conv(blocks, tables, parts, chunk, repeats, orient, last, joined)

    def shaped(blocks, shape):
        return [block.reshape(shape) for block in blocks]

    early, late = halves(peers)
    first_group, second_group = early + late[:1], late[1:]
    flat = (chunks, shard_rows * rows, width)

    mixed = [None] * peers
    last = pos
    grid, tok_spec, part_spec = specs(16)
    for group in (first_group, second_group):
        some = len(group) * chunks * rows
        outs = pl.pallas_call(
            functools.partial(mixed_kernel, peers=peers, blocks=group),
            grid=grid,
            in_specs=[POS_SPEC, tok_spec, w_spec, pick_spec],
            out_specs=[part_spec] * len(group),
            out_shape=[part_out] * len(group),
            scratch_shapes=[held(some), held(2 * some)],
            compiler_params=params(),
            cost_estimate=cost(1, 1.5),
            name="mixed",
        )(last, tokens, w_in, pick)
        last, outs = after(list(outs), pos)
        for block, out in zip(group, outs):
            mixed[block] = out
    own = own_filters(filter_real, filter_imag, peers, lax.axis_size("dp"), group_pos)
    own, mixed[0] = after(mixed[0], own)
    mine = exchange(own)
    arrived = send(send(mixed, first_group), second_group)
    (last, mine), held_back = after([arrived[block] for block in early], (last, mine))
    for block, value in zip(early, held_back):
        arrived[block] = value
    grid, tok_spec, part_spec = specs(8)
    grads = list(pl.pallas_call(
        functools.partial(grad_kernel, peers=peers),
        grid=grid,
        in_specs=[POS_SPEC, tok_spec, tok_spec, w_spec, pick_spec],
        out_specs=[part_spec] * peers,
        out_shape=[part_out] * peers,
        scratch_shapes=[held(chan), held(chan)],
        compiler_params=params(),
        cost_estimate=cost(2, 3),
        name="grad_smooth",
    )(last, tokens, cotangent, w_in, pick))
    parts = lax.all_gather(mine, "dp", axis=0, tiled=False)

    arrived = shaped(arrived, flat)
    grads = shaped(grads, flat)
    joined = conv(arrived, 0, 1.0, pos, [])
    grads = send(grads, early)
    (last, grads), joined = after(joined, (pos, grads))
    joined = conv(arrived, 1, 1.0, last, joined)
    grads = send(grads, late)
    last, joined = after(joined, pos)
    back = conv(grads, 0, -1.0, last, [])
    smooth = send(joined, early)
    (last, smooth), back = after(back, (pos, smooth))
    back = conv(grads, 1, -1.0, last, back)
    smooth = send(smooth, late)
    last, back = after(back, pos)
    back = send(back, early)

    def kept(cols):
        shape = (groups, chan // groups // 2, cols)
        return (
            [pl.BlockSpec(shape, lambda i: (0, 0, 0))] * 2, [jax.ShapeDtypeStruct(shape, F32)] * 2
        )

    kept_specs, kept_shapes = kept(chan)
    gated, *gate_sum = pl.pallas_call(
        smooth_kernel,
        grid=grid,
        in_specs=[POS_SPEC, tok_spec, tok_spec, w_spec, pick_spec] + [part_spec] * peers,
        out_specs=[tok_spec] + kept_specs,
        out_shape=[jax.ShapeDtypeStruct((tok_rows, chan), BF)] + kept_shapes,
        scratch_shapes=[held(chan), held(chan), held(chan, F32), held(chan, F32)],
        compiler_params=params(),
        cost_estimate=cost(4, 4),
        name="smooth",
    )(last, tokens, cotangent, w_in, pick, *shaped(smooth, part_out.shape))
    back, gate_sum = after(gate_sum, back)
    gate_sum = reduce_kept(*gate_sum)
    last, gate_sum = after(gate_sum, pos)
    back = send(back, late)

    sum_shape = (chan, 2 * chan)
    grid, tok_spec, part_spec = specs(8)
    some, others = len(early) * chunks * rows, len(late) * chunks * rows
    steps = tok_spec.block_shape[0]
    feat_spec = pl.BlockSpec((2 * others, steps), lambda i: (0, i))
    back_sum, feats = pl.pallas_call(
        functools.partial(back_first_kernel, peers=peers, blocks=early, others=late),
        grid=grid,
        in_specs=[POS_SPEC, tok_spec, w_spec, pick_spec] + [part_spec] * len(early),
        out_specs=[pl.BlockSpec(sum_shape, lambda i: (0, 0)), feat_spec],
        out_shape=[
            jax.ShapeDtypeStruct(sum_shape, F32),
            jax.ShapeDtypeStruct((2 * others, tok_rows), BF),
        ],
        scratch_shapes=[
            held(some), held(others), held(2 * (some + others)), held(2 * some, F32),
            held(2 * chan, F32),
        ],
        compiler_params=params(),
        cost_estimate=cost(3, 3),
        name="back_first",
    )(last, tokens, w_in, pick, *shaped([back[block] for block in early], part_out.shape))
    kept_specs, kept_shapes = kept(2 * chan)
    back_sum = pl.pallas_call(
        functools.partial(back_last_kernel, peers=peers, blocks=late),
        grid=grid,
        in_specs=[POS_SPEC, tok_spec, feat_spec, whole(sum_shape)] + [part_spec] * len(late),
        out_specs=kept_specs,
        out_shape=kept_shapes,
        scratch_shapes=[
            held(2 * others, F32), held(2 * chan, F32), pltpu.VMEM(sum_shape, F32)
        ],
        compiler_params=params(),
        cost_estimate=cost(1, 2.5),
        name="back_last",
    )(pos, tokens, feats, back_sum, *shaped([back[block] for block in late], part_out.shape))
    summed = jnp.concatenate([gate_sum, reduce_kept(*back_sum)], axis=1)
    return gated, reduce_chips(summed)


def without_kernels(arrays, tables, pick, rows, repeats, group_pos):
    tokens, cotangent, w_in, filter_real, filter_imag = arrays
    peers = lax.axis_size("ctx")
    tok_rows, chan = tokens.shape
    width = tables[4].shape[1]
    shard_rows = tok_rows // width
    wt = [
        dot_nt(pick, w_in[:, part * chan : (part + 1) * chan]).astype(BF) for part in range(3)
    ]
    gate, key, value = [dot_nt(block, tokens).astype(BF).astype(F32) for block in wt]
    cot = dot_nt(pick, cotangent)
    own = own_filters(filter_real, filter_imag, peers, lax.axis_size("dp"), group_pos)
    parts = gather_filters(own)
    groups, _, each, _, quarter, _ = parts.shape
    filt = parts.transpose(3, 2, 1, 0, 4, 5).reshape(2, each, peers * groups * quarter, width)

    def convolved(array, orient):
        array = array.astype(BF).reshape(peers, rows, shard_rows, width).transpose(0, 2, 1, 3)
        result = run_conv_plain(exchange(array), tables, (filt[0], filt[1]), repeats, orient)
        result = exchange(result).transpose(0, 2, 1, 3)
        return result.reshape(chan, tok_rows).astype(F32)

    smooth = convolved(key * value, 1.0)
    back = convolved(gate * cot, -1.0)
    gated = dot_tn((gate * smooth).astype(BF), pick).astype(BF)
    terms = [cot * smooth, back * value, back * key]
    sums = [dot_nn(term.astype(BF), tokens).T for term in terms]
    summed = reduce_tokens(reduce_groups(jnp.concatenate(sums, axis=1)))
    return gated, summed


def per_device(inputs, grad_out, w_in, filter_real, filter_imag):
    ctx_count = lax.axis_size("ctx")
    group_count = lax.axis_size("dp")
    tokens = inputs[0]
    cotangent = grad_out[0]
    tok_rows, chan_total = tokens.shape
    chan_half = chan_total // 2
    n_one = filter_real.shape[0] * ctx_count
    n_two = filter_real.shape[1]
    filters = filter_real.shape[2]
    repeats = chan_half // filters
    seq_len = n_one * n_two // 2
    shard_rows = tok_rows // n_two
    per_device_chan = chan_half // ctx_count
    quarter = filter_real.shape[0] // group_count
    use_kernels = (
        per_device_chan % 16 == 0 and quarter % 16 == 0 and repeats % (per_device_chan // 2) == 0
        and ctx_count & (ctx_count - 1) == 0
    )
    chunks = 2 if use_kernels else 1
    rows = 2 * (per_device_chan // chunks)

    tables = tuple(jnp.asarray(table) for table in transform_tables(n_one, n_two))
    order = channel_order(chan_half, filters, ctx_count, chunks)
    pick_np = np.zeros((chan_total, chan_total), np.float32)
    pick_np[np.arange(chan_total), order] = 1.0
    pick = jnp.asarray(pick_np.astype(ml_dtypes.bfloat16))
    group_pos = lax.axis_index("dp")
    arrays = (tokens, cotangent, w_in, filter_real, filter_imag)
    if use_kernels:
        gated, summed = with_kernels(
            arrays, tables, pick, chunks, repeats, group_pos
        )
    else:
        gated, summed = without_kernels(
            arrays, tables, pick, rows, repeats, group_pos
        )

    scale = 1.0 / math.sqrt(inputs.shape[0] * group_count * seq_len)

    ordered = jnp.dot(
        summed.reshape(-1, chan_total), pick.astype(F32), precision=lax.Precision.HIGHEST
    )
    summed = ordered.reshape(summed.shape)
    return (gated[None], summed * scale)


def solution(mesh):
    placed = (
        P("dp", "ctx", None),
        P("dp", "ctx", None),
        P(),
        P("ctx", None, None),
        P("ctx", None, None),
    )
    return jax.shard_map(
        per_device,
        mesh=mesh,
        in_specs=placed,
        out_specs=(P("dp", "ctx", None), P("dp", None)),
        check_vma=False,
    )
```

```python
import functools
import math

import jax
import jax.numpy as jnp
import ml_dtypes
import numpy as np
from jax import lax
from jax.experimental import pallas as pl
from jax.experimental.pallas import tpu as pltpu
from jax.sharding import PartitionSpec as P

BF = jnp.bfloat16
F32 = jnp.float32
VMEM_BYTES = 60 * 1024 * 1024
POS_SPEC = pl.BlockSpec(memory_space=pltpu.SMEM)


def dot_nn(left, right):
    return lax.dot_general(left, right, (((1,), (0,)), ((), ())), preferred_element_type=F32)


def dot_nt(left, right):
    return lax.dot_general(left, right, (((1,), (1,)), ((), ())), preferred_element_type=F32)


def dot_tn(left, right):
    return lax.dot_general(left, right, (((0,), (0,)), ((), ())), preferred_element_type=F32)


def rounded(value):
    return value.astype(BF).astype(F32)


def transform_tables(n_one, n_two):
    def table(rows, cols, period):
        angle = (np.arange(rows)[:, None] * np.arange(cols)[None, :] % period) * (
            2.0 * math.pi / period
        )
        factor = 1.0 / math.sqrt(period)
        return (
            (np.cos(angle) * factor).astype(np.float32).astype(ml_dtypes.bfloat16),
            (np.sin(angle) * factor).astype(np.float32).astype(ml_dtypes.bfloat16),
        )

    cos_one, sin_one = table(n_one, n_one // 2, n_one)
    cos_two, sin_two = table(n_two, n_two, n_two)
    period = n_one * n_two
    angle = (np.arange(n_one)[:, None] * np.arange(n_two)[None, :] % period) * (
        2.0 * math.pi / period
    )
    first = np.block([[cos_one, sin_one], [-sin_one, cos_one]])
    second = np.block([[cos_two, -sin_two], [sin_two, cos_two]])
    third = np.block([[cos_two, sin_two], [-sin_two, cos_two]])
    fourth = np.block([[cos_one.T, -sin_one.T], [sin_one.T, cos_one.T]])
    return (
        first,
        second,
        third,
        fourth,
        np.cos(angle).astype(np.float32),
        np.sin(angle).astype(np.float32),
    )


def channel_order(chan_half, filters, ctx_count, chunks):
    repeats = chan_half // filters
    per_device = chan_half // ctx_count
    per_chunk = per_device // chunks
    order = []
    for chunk in range(chunks):
        for device in range(ctx_count):
            for part in range(2):
                for place in range(per_chunk):
                    index = device * per_device + chunk * per_chunk + place
                    group, repeat = divmod(index, repeats)
                    order.append(part * chan_half + repeat * filters + group)
    return np.array(order)


def gather_rows(pos_ref, pick_ref, held_ref, peers, blocks, rows):
    pos = pos_ref[0]
    chunks = pick_ref.shape[0] // (peers * rows)
    spot = 0
    for block in blocks:
        for chunk in range(chunks):
            start = pl.multiple_of((chunk * peers + (pos ^ block)) * rows, rows)
            held_ref[spot : spot + rows, :] = pick_ref[pl.ds(start, rows), :]
            spot += rows


def key_value_weights(w_ref, held_ref, wt_ref):
    count, chan = held_ref.shape
    for part in range(2):
        block = w_ref[:, (1 + part) * chan : (2 + part) * chan]
        wt_ref[part * count : (part + 1) * count, :] = dot_nt(held_ref[...], block).astype(BF)


def store_blocks(value, outs, step):
    chunks, _, rows, _ = outs[0].shape
    spot = 0
    for out in outs:
        for chunk in range(chunks):
            out[chunk, step] = value[spot : spot + rows]
            spot += rows


def load_blocks(parts, step):
    chunks = parts[0].shape[0]
    return jnp.concatenate(
        [part[chunk, step] for part in parts for chunk in range(chunks)], axis=0
    ).astype(F32)


def mixed_kernel(pos_ref, tok_ref, w_ref, pick_ref, *rest, peers, blocks):
    outs, (held_ref, wt_ref) = rest[:-2], rest[-2:]
    _, steps, rows, width = outs[0].shape
    count = held_ref.shape[0]

    @pl.when(pl.program_id(0) == 0)
    def _():
        gather_rows(pos_ref, pick_ref, held_ref, peers, blocks, rows)
        key_value_weights(w_ref, held_ref, wt_ref)

    for step in range(steps):
        feats = rounded(dot_nt(wt_ref[...], tok_ref[step * width : (step + 1) * width, :]))
        store_blocks((feats[:count] * feats[count:]).astype(BF), outs, step)


def grad_kernel(pos_ref, tok_ref, cot_ref, w_ref, pick_ref, *rest, peers):
    outs, (held_ref, wt_ref) = rest[:-2], rest[-2:]
    _, steps, rows, width = outs[0].shape
    chan = pick_ref.shape[1]

    @pl.when(pl.program_id(0) == 0)
    def _():
        gather_rows(pos_ref, pick_ref, held_ref, peers, range(peers), rows)
        wt_ref[...] = dot_nt(held_ref[...], w_ref[:, :chan]).astype(BF)

    for step in range(steps):
        span = slice(step * width, (step + 1) * width)
        gate = rounded(dot_nt(wt_ref[...], tok_ref[span, :]))
        cot = dot_nt(held_ref[...], cot_ref[span, :])
        store_blocks((gate * cot).astype(BF), outs, step)


def convolve(signal, refs, filt_real, filt_imag, orient, hold_ref):
    first_ref, second_ref, third_ref, fourth_ref, cos_ref, sin_ref = refs
    n_one, n_two = cos_ref.shape
    cos, sin = cos_ref[...], sin_ref[...]
    partial = dot_nn(first_ref[...], signal)
    real, imag = partial[:n_one], partial[n_one:]
    turned = jnp.concatenate(
        [(real * cos + imag * sin).astype(BF), (imag * cos - real * sin).astype(BF)], axis=1
    )
    spec = dot_nn(turned, second_ref[...])
    real, imag = spec[:, :n_two], spec[:, n_two:]
    f_real = filt_real.astype(F32)
    f_imag = filt_imag.astype(F32) * orient
    product = jnp.concatenate(
        [
            (real * f_real - imag * f_imag).astype(BF),
            (real * f_imag + imag * f_real).astype(BF),
        ],
        axis=1,
    )
    back = dot_nn(product, third_ref[...])
    real, imag = back[:, :n_two], back[:, n_two:]
    hold_ref[:n_one, :] = (real * cos - imag * sin).astype(BF)
    hold_ref[n_one:, :] = (imag * cos + real * sin).astype(BF)
    return dot_nn(fourth_ref[...], hold_ref[...])


def conv_kernel(pos_ref, *args, peers, rows, orient):
    ins, rest = args[:peers], args[peers:]
    tables, rest = rest[:6], rest[6:]
    parts_ref, rest = rest[0], rest[1:]
    outs, (in_ref, res_ref, hold_ref, filt_ref) = rest[-4 - peers : -4], rest[-4:]
    lanes = 128
    _, size, width = ins[0].shape
    times = peers * size // rows
    half = rows // 2
    place = pl.program_id(0)
    pos = pos_ref[0]
    piece = math.gcd(size, 256)

    @pl.when(place == 0)
    def _():
        groups, _, _, _, quarter, _ = parts_ref.shape
        for block in range(peers):
            base = (pos ^ block) * size
            for group in range(groups):
                start = (block * groups + group) * quarter
                span = slice(start, start + quarter)
                for part in range(2):
                    filt_ref[part, span, :] = parts_ref[group, block, 0, part]

            @pl.loop(0, size // piece)
            def _(index):
                wide = ins[block][0, pl.ds(pl.multiple_of(index * piece, piece), piece), :]
                wide = wide.astype(F32)
                span = pl.ds(pl.multiple_of(base + index * piece, piece), piece)
                for lane in range(width // lanes):
                    in_ref[lane, span, :] = wide[:, lane * lanes : (lane + 1) * lanes]

    parts = []
    for part in range(2):
        columns = [
            in_ref[lane, pl.ds(place + part * half, times, stride=rows), :].astype(BF)
            for lane in range(width // lanes)
        ]
        parts.append(jnp.concatenate(columns, axis=1))
    signal = jnp.concatenate(parts, axis=0)
    result = convolve(
        signal,
        tables,
        filt_ref[0],
        filt_ref[1],
        orient,
        hold_ref,
    )
    for part in range(2):
        for lane in range(width // lanes):
            res_ref[lane, pl.ds(place + part * half, times, stride=rows), :] = result[
                part * times : (part + 1) * times, lane * lanes : (lane + 1) * lanes
            ]

    @pl.when(place == pl.num_programs(0) - 1)
    def _():
        for block in range(peers):
            base = (pos ^ block) * size

            @pl.loop(0, size // piece)
            def _(index):
                span = pl.ds(pl.multiple_of(base + index * piece, piece), piece)
                outs[block][0, pl.ds(pl.multiple_of(index * piece, piece), piece), :] = (
                    jnp.concatenate(
                        [res_ref[lane, span, :] for lane in range(width // lanes)], axis=1
                    ).astype(BF)
                )


def conv_plain_kernel(x_ref, first, second, third, fourth, cos, sin, fr_ref, fi_ref, out_ref,
                      hold_ref, *, orient):
    out_ref[0] = convolve(
        x_ref[0],
        (first, second, third, fourth, cos, sin),
        fr_ref[0],
        fi_ref[0],
        orient,
        hold_ref,
    ).astype(BF)


def whole(shape):
    zeros = (0,) * len(shape)
    return pl.BlockSpec(shape, lambda *_: zeros, pipeline_mode=pl.Buffered(1))


def params():
    return pltpu.CompilerParams(
        dimension_semantics=("arbitrary",), vmem_limit_bytes=VMEM_BYTES
    )


def conv_cost(count, n_one, n_two, moved):
    macs = count * 2 * (n_one * n_one * n_two + 2 * n_one * n_two * n_two)
    return pl.CostEstimate(flops=2 * macs, bytes_accessed=moved, transcendentals=0)


def run_conv(blocks, tables, parts, chunk, repeats, orient, pos, joined):
    peers = len(blocks)
    chunks, size, width = blocks[0].shape
    n_one, n_two = tables[4].shape
    rows = size * peers // (n_one // 2)
    half = rows // 2
    table_specs = [whole(table.shape) for table in tables]
    block_spec = pl.BlockSpec(
        (1, size, width), lambda place: (chunk, 0, 0), pipeline_mode=pl.Buffered(1)
    )
    parts_shape = parts.shape[:2] + (1,) + parts.shape[3:]
    place_of = (0, 0, chunk * half // repeats, 0, 0, 0)
    parts_spec = pl.BlockSpec(
        parts_shape, lambda place: place_of, pipeline_mode=pl.Buffered(1)
    )
    moved = 4 * peers * size * width
    moved += sum(table.size * table.dtype.itemsize for table in tables)
    slots = pltpu.VMEM((width // 128, peers * size, 128), F32)
    first = 1 + peers + len(tables) + 1
    out_spec = pl.BlockSpec((1, size, width), lambda place: (chunk, 0, 0))
    return list(pl.pallas_call(
        functools.partial(conv_kernel, peers=peers, rows=rows, orient=orient),
        grid=(half,),
        in_specs=[POS_SPEC] + [block_spec] * peers + table_specs + [parts_spec]
        + [pl.BlockSpec(memory_space=pl.ANY)] * len(joined),
        out_specs=[out_spec] * peers,
        out_shape=[jax.ShapeDtypeStruct((chunks, size, width), BF)] * peers,
        input_output_aliases={first + index: index for index in range(len(joined))},
        scratch_shapes=[
            slots, slots, pltpu.VMEM((2 * n_one, n_two), BF), pltpu.VMEM((2, n_one, n_two), BF)
        ],
        compiler_params=params(),
        cost_estimate=conv_cost(half, n_one, n_two, moved),
        name="conv",
    )(pos, *blocks, *tables, parts, *joined))


def run_conv_plain(blocks, tables, filt, repeats, orient):
    sources, shard_rows, rows, width = blocks.shape
    n_one, n_two = tables[4].shape
    times = sources * shard_rows
    half = rows // 2
    filters = filt[0].shape[0]
    filt_spec = pl.BlockSpec(
        (1, n_one, n_two), lambda place: (jnp.minimum(place // repeats, filters - 1), 0, 0)
    )
    moved = 4 * blocks.size
    signal = blocks.reshape(times, 2, half, width).transpose(2, 1, 0, 3)
    signal = signal.reshape(half, 2 * times, width)
    channel_spec = pl.BlockSpec((1, 2 * times, width), lambda place: (place, 0, 0))
    result = pl.pallas_call(
        functools.partial(conv_plain_kernel, orient=orient),
        grid=(half,),
        in_specs=[channel_spec] + [whole(table.shape) for table in tables] + [filt_spec] * 2,
        out_specs=channel_spec,
        out_shape=jax.ShapeDtypeStruct(signal.shape, BF),
        scratch_shapes=[pltpu.VMEM((2 * n_one, n_two), BF)],
        compiler_params=params(),
        cost_estimate=conv_cost(half, n_one, n_two, moved),
        name="conv_plain",
    )(signal, *tables, *filt)
    result = result.reshape(half, 2, times, width).transpose(2, 1, 0, 3)
    return result.reshape(blocks.shape)


def store_sum(pos_ref, total, outs, turn_ref, flat_ref, peers, blocks, chunks, rows, earlier):
    pos = pos_ref[0]
    kinds = total.shape[0] // (len(blocks) * chunks * rows)
    spot = 0
    if len(blocks) < peers:
        turn_ref[...] = jnp.zeros_like(turn_ref)
    for kind in range(kinds):
        for block in blocks:
            for chunk in range(chunks):
                start = ((kind * chunks + chunk) * peers + (pos ^ block)) * rows
                span = pl.ds(pl.multiple_of(start, rows), rows)
                turn_ref[span, :] = total[spot : spot + rows]
                spot += rows
    summed = turn_ref[...].T
    for ref in earlier:
        summed = summed + ref[...]
    if len(outs) == 1:
        outs[0][...] = summed
        return
    flat_ref[...] = summed
    keep_ref, sent_ref = outs
    groups, size, _ = keep_ref.shape
    core = pos % 2
    for group in range(groups):
        base = lax.rem(pos_ref[1] + group, groups) * (2 * size)
        keep_ref[group] = flat_ref[pl.ds(pl.multiple_of(base + core * size, size), size), :]
        sent_ref[group] = flat_ref[pl.ds(pl.multiple_of(base + (1 - core) * size, size), size), :]


def smooth_kernel(pos_ref, tok_ref, cot_ref, w_ref, pick_ref, *rest):
    parts, (gated_ref, *outs) = rest[:-7], rest[-7:-4]
    held_ref, wt_ref, total_ref, turn_ref = rest[-4:]
    chunks, steps, rows, width = parts[0].shape
    peers = len(parts)
    chan = pick_ref.shape[1]

    @pl.when(pl.program_id(0) == 0)
    def _():
        gather_rows(pos_ref, pick_ref, held_ref, peers, range(peers), rows)
        wt_ref[...] = dot_nt(held_ref[...], w_ref[:, :chan]).astype(BF)
        total_ref[...] = jnp.zeros_like(total_ref)

    total = total_ref[...]
    for step in range(steps):
        span = slice(step * width, (step + 1) * width)
        tokens = tok_ref[span, :]
        gate = rounded(dot_nt(wt_ref[...], tokens))
        cot = dot_nt(held_ref[...], cot_ref[span, :])
        smooth = load_blocks(parts, step)
        gated_ref[span, :] = dot_tn((gate * smooth).astype(BF), held_ref[...]).astype(BF)
        total = total + dot_nn((cot * smooth).astype(BF), tokens)
    total_ref[...] = total

    @pl.when(pl.program_id(0) == pl.num_programs(0) - 1)
    def _():
        store_sum(
            pos_ref, total, outs, turn_ref, total_ref, peers, range(peers), chunks, rows, []
        )


def back_terms(parts, feats, tokens, step):
    count = feats.shape[0] // 2
    mixed = load_blocks(parts, step)
    grads = [mixed * feats[count:], mixed * feats[:count]]
    return dot_nn(jnp.concatenate([grad.astype(BF) for grad in grads], axis=0), tokens)


def back_first_kernel(pos_ref, tok_ref, w_ref, pick_ref, *rest, peers, blocks, others):
    parts, (sum_ref, feat_ref) = rest[: len(blocks)], rest[len(blocks) : -5]
    held_ref, later_ref, wt_ref, total_ref, turn_ref = rest[-5:]
    chunks, steps, rows, width = parts[0].shape
    count = 2 * held_ref.shape[0]

    @pl.when(pl.program_id(0) == 0)
    def _():
        gather_rows(pos_ref, pick_ref, held_ref, peers, blocks, rows)
        gather_rows(pos_ref, pick_ref, later_ref, peers, others, rows)
        key_value_weights(w_ref, held_ref, wt_ref.at[:count])
        key_value_weights(w_ref, later_ref, wt_ref.at[count:])
        total_ref[...] = jnp.zeros_like(total_ref)

    total = total_ref[...]
    for step in range(steps):
        span = slice(step * width, (step + 1) * width)
        tokens = tok_ref[span, :]
        feats = dot_nt(wt_ref[...], tokens).astype(BF)
        feat_ref[:, span] = feats[count:]
        total = total + back_terms(parts, feats[:count].astype(F32), tokens, step)
    total_ref[...] = total

    @pl.when(pl.program_id(0) == pl.num_programs(0) - 1)
    def _():
        store_sum(
            pos_ref, total, [sum_ref], turn_ref, None, peers, blocks, chunks, rows, []
        )


def back_last_kernel(pos_ref, tok_ref, feat_ref, earlier_ref, *rest, peers, blocks):
    parts, outs = rest[: len(blocks)], rest[len(blocks) : -3]
    total_ref, turn_ref, flat_ref = rest[-3:]
    chunks, steps, rows, width = parts[0].shape

    @pl.when(pl.program_id(0) == 0)
    def _():
        total_ref[...] = jnp.zeros_like(total_ref)

    total = total_ref[...]
    for step in range(steps):
        span = slice(step * width, (step + 1) * width)
        feats = feat_ref[:, span].astype(F32)
        total = total + back_terms(parts, feats, tok_ref[span, :], step)
    total_ref[...] = total

    @pl.when(pl.program_id(0) == pl.num_programs(0) - 1)
    def _():
        store_sum(
            pos_ref, total, outs, turn_ref, flat_ref, peers, blocks, chunks, rows, [earlier_ref]
        )


def halves(peers):
    order = [block for block in range(2, peers, 2)] + [block for block in range(3, peers, 2)]
    return tuple(order[: peers // 2 - 1]), tuple(order[peers // 2 - 1 :] + [1, 0])


def send(blocks, group):
    arrived = list(blocks)
    peers = len(blocks)
    for block in group:
        if block:
            pairs = [(device, device ^ block) for device in range(peers)]
            arrived[block] = lax.ppermute(blocks[block], "ctx", pairs)
    return arrived


def exchange(blocks):
    return lax.all_to_all(blocks, "ctx", split_axis=0, concat_axis=0, tiled=True)


def own_filters(filter_real, filter_imag, ctx_count, group_count, group_pos):
    rows, n_two, filters = filter_real.shape
    quarter = rows // group_count
    own = lax.dynamic_slice_in_dim(
        jnp.stack([filter_real, filter_imag]), group_pos * quarter, quarter, 1
    )
    own = own.astype(BF).transpose(3, 0, 1, 2)
    if ctx_count > filters:
        own = jnp.repeat(own, ctx_count // filters, axis=0)
    return own.reshape(ctx_count, own.shape[0] // ctx_count, 2, quarter, n_two)


def gather_filters(own):
    return lax.all_gather(exchange(own), "dp", axis=0, tiled=False)


def after(first, value):
    return lax.optimization_barrier((value, first))


def reduce_groups(value):
    count = lax.axis_size("dp")
    pos = lax.axis_index("dp")
    split = value.reshape(count, value.shape[0] // count, value.shape[1])
    total = lax.dynamic_index_in_dim(split, pos, 0, keepdims=False)
    for step in range(1, count):
        pairs = [(device, (device + step) % count) for device in range(count)]
        sent = lax.dynamic_index_in_dim(split, (pos + step) % count, 0, keepdims=False)
        total = total + lax.ppermute(sent, "dp", pairs)
    return total


def reduce_tokens(value):
    count = lax.axis_size("ctx")
    step = 1
    while step < count:
        pairs = [(device, device ^ step) for device in range(count)]
        value = value + lax.ppermute(value, "ctx", pairs)
        step *= 2
    return value


def swap(value, step):
    pairs = [(device, device ^ step) for device in range(lax.axis_size("ctx"))]
    return lax.ppermute(value, "ctx", pairs)


def reduce_kept(keep, sent):
    keep = keep + swap(sent, 1)
    groups = lax.axis_size("dp")
    total = keep[0]
    for step in range(1, groups):
        pairs = [(device, (device + step) % groups) for device in range(groups)]
        total = total + lax.ppermute(keep[step], "dp", pairs)
    return total


def reduce_chips(total):
    terms = [total] + [swap(total, step) for step in range(2, lax.axis_size("ctx"), 2)]
    while len(terms) > 1:
        terms = [left + right for left, right in zip(terms[::2], terms[1::2])]
    total = terms[0]
    other = swap(total, 1)
    upper = lax.axis_index("ctx") % 2 != 0
    return jnp.concatenate([jnp.where(upper, other, total), jnp.where(upper, total, other)])


def with_kernels(arrays, tables, pick, chunks, repeats, group_pos):
    tokens, cotangent, w_in, filter_real, filter_imag = arrays
    peers = lax.axis_size("ctx")
    tok_rows, chan = tokens.shape
    width = tables[4].shape[1]
    shard_rows = tok_rows // width
    rows = chan // (peers * chunks)
    count = peers * rows
    me = lax.axis_index("ctx").astype(jnp.int32)
    pos = jnp.stack([me, group_pos.astype(jnp.int32)])
    groups = lax.axis_size("dp")

    def specs(most):
        steps = math.gcd(shard_rows, most)
        return (
            (shard_rows // steps,),
            pl.BlockSpec((steps * width, chan), lambda i: (i, 0)),
            pl.BlockSpec((chunks, steps, rows, width), lambda i: (0, i, 0, 0)),
        )

    part_out = jax.ShapeDtypeStruct((chunks, shard_rows, rows, width), BF)
    w_spec, pick_spec = whole(w_in.shape), whole(pick.shape)
    macs = tok_rows * chan * chan

    def held(count, kind=BF):
        return pltpu.VMEM((count, chan), kind)

    def cost(times, moved):
        return pl.CostEstimate(
            flops=int(2 * macs * times), bytes_accessed=int(moved * 2 * tok_rows * chan),
            transcendentals=0,
        )

    def conv(blocks, chunk, orient, last, joined):
        return run_conv(blocks, tables, parts, chunk, repeats, orient, last, joined)

    def shaped(blocks, shape):
        return [block.reshape(shape) for block in blocks]

    early, late = halves(peers)
    first_group, second_group = early + late[:1], late[1:]
    flat = (chunks, shard_rows * rows, width)

    mixed = [None] * peers
    last = pos
    grid, tok_spec, part_spec = specs(16)
    for group in (first_group, second_group):
        some = len(group) * chunks * rows
        outs = pl.pallas_call(
            functools.partial(mixed_kernel, peers=peers, blocks=group),
            grid=grid,
            in_specs=[POS_SPEC, tok_spec, w_spec, pick_spec],
            out_specs=[part_spec] * len(group),
            out_shape=[part_out] * len(group),
            scratch_shapes=[held(some), held(2 * some)],
            compiler_params=params(),
            cost_estimate=cost(1, 1.5),
            name="mixed",
        )(last, tokens, w_in, pick)
        last, outs = after(list(outs), pos)
        for block, out in zip(group, outs):
            mixed[block] = out
    own = own_filters(filter_real, filter_imag, peers, lax.axis_size("dp"), group_pos)
    own, mixed[0] = after(mixed[0], own)
    mine = exchange(own)
    arrived = send(send(mixed, first_group), second_group)
    (last, mine), held_back = after([arrived[block] for block in early], (last, mine))
    for block, value in zip(early, held_back):
        arrived[block] = value
    grid, tok_spec, part_spec = specs(8)
    grads = list(pl.pallas_call(
        functools.partial(grad_kernel, peers=peers),
        grid=grid,
        in_specs=[POS_SPEC, tok_spec, tok_spec, w_spec, pick_spec],
        out_specs=[part_spec] * peers,
        out_shape=[part_out] * peers,
        scratch_shapes=[held(chan), held(chan)],
        compiler_params=params(),
        cost_estimate=cost(2, 3),
        name="grad_smooth",
    )(last, tokens, cotangent, w_in, pick))
    parts = lax.all_gather(mine, "dp", axis=0, tiled=False)

    arrived = shaped(arrived, flat)
    grads = shaped(grads, flat)
    joined = conv(arrived, 0, 1.0, pos, [])
    grads = send(grads, early)
    (last, grads), joined = after(joined, (pos, grads))
    joined = conv(arrived, 1, 1.0, last, joined)
    grads = send(grads, late)
    last, joined = after(joined, pos)
    back = conv(grads, 0, -1.0, last, [])
    smooth = send(joined, early)
    (last, smooth), back = after(back, (pos, smooth))
    back = conv(grads, 1, -1.0, last, back)
    smooth = send(smooth, late)
    last, back = after(back, pos)
    early, late = early + (1, 0), late[:-2]
    back = send(back, early)

    def kept(cols):
        shape = (groups, chan // groups // 2, cols)
        return (
            [pl.BlockSpec(shape, lambda i: (0, 0, 0))] * 2, [jax.ShapeDtypeStruct(shape, F32)] * 2
        )

    kept_specs, kept_shapes = kept(chan)
    gated, *gate_sum = pl.pallas_call(
        smooth_kernel,
        grid=grid,
        in_specs=[POS_SPEC, tok_spec, tok_spec, w_spec, pick_spec] + [part_spec] * peers,
        out_specs=[tok_spec] + kept_specs,
        out_shape=[jax.ShapeDtypeStruct((tok_rows, chan), BF)] + kept_shapes,
        scratch_shapes=[held(chan), held(chan), held(chan, F32), held(chan, F32)],
        compiler_params=params(),
        cost_estimate=cost(4, 4),
        name="smooth",
    )(last, tokens, cotangent, w_in, pick, *shaped(smooth, part_out.shape))
    back, gate_sum = after(gate_sum, back)
    gate_sum = reduce_kept(*gate_sum)
    last, gate_sum = after(gate_sum, pos)
    back = send(back, late)

    sum_shape = (chan, 2 * chan)
    grid, tok_spec, part_spec = specs(8)
    some, others = len(early) * chunks * rows, len(late) * chunks * rows
    steps = tok_spec.block_shape[0]
    feat_spec = pl.BlockSpec((2 * others, steps), lambda i: (0, i))
    back_sum, feats = pl.pallas_call(
        functools.partial(back_first_kernel, peers=peers, blocks=early, others=late),
        grid=grid,
        in_specs=[POS_SPEC, tok_spec, w_spec, pick_spec] + [part_spec] * len(early),
        out_specs=[pl.BlockSpec(sum_shape, lambda i: (0, 0)), feat_spec],
        out_shape=[
            jax.ShapeDtypeStruct(sum_shape, F32),
            jax.ShapeDtypeStruct((2 * others, tok_rows), BF),
        ],
        scratch_shapes=[
            held(some), held(others), held(2 * (some + others)), held(2 * some, F32),
            held(2 * chan, F32),
        ],
        compiler_params=params(),
        cost_estimate=cost(3, 3),
        name="back_first",
    )(last, tokens, w_in, pick, *shaped([back[block] for block in early], part_out.shape))
    kept_specs, kept_shapes = kept(2 * chan)
    back_sum = pl.pallas_call(
        functools.partial(back_last_kernel, peers=peers, blocks=late),
        grid=grid,
        in_specs=[POS_SPEC, tok_spec, feat_spec, whole(sum_shape)] + [part_spec] * len(late),
        out_specs=kept_specs,
        out_shape=kept_shapes,
        scratch_shapes=[
            held(2 * others, F32), held(2 * chan, F32), pltpu.VMEM(sum_shape, F32)
        ],
        compiler_params=params(),
        cost_estimate=cost(1, 2.5),
        name="back_last",
    )(pos, tokens, feats, back_sum, *shaped([back[block] for block in late], part_out.shape))
    summed = jnp.concatenate([gate_sum, reduce_kept(*back_sum)], axis=1)
    return gated, reduce_chips(summed)


def without_kernels(arrays, tables, pick, rows, repeats, group_pos):
    tokens, cotangent, w_in, filter_real, filter_imag = arrays
    peers = lax.axis_size("ctx")
    tok_rows, chan = tokens.shape
    width = tables[4].shape[1]
    shard_rows = tok_rows // width
    wt = [
        dot_nt(pick, w_in[:, part * chan : (part + 1) * chan]).astype(BF) for part in range(3)
    ]
    gate, key, value = [dot_nt(block, tokens).astype(BF).astype(F32) for block in wt]
    cot = dot_nt(pick, cotangent)
    own = own_filters(filter_real, filter_imag, peers, lax.axis_size("dp"), group_pos)
    parts = gather_filters(own)
    groups, _, each, _, quarter, _ = parts.shape
    filt = parts.transpose(3, 2, 1, 0, 4, 5).reshape(2, each, peers * groups * quarter, width)

    def convolved(array, orient):
        array = array.astype(BF).reshape(peers, rows, shard_rows, width).transpose(0, 2, 1, 3)
        result = run_conv_plain(exchange(array), tables, (filt[0], filt[1]), repeats, orient)
        result = exchange(result).transpose(0, 2, 1, 3)
        return result.reshape(chan, tok_rows).astype(F32)

    smooth = convolved(key * value, 1.0)
    back = convolved(gate * cot, -1.0)
    gated = dot_tn((gate * smooth).astype(BF), pick).astype(BF)
    terms = [cot * smooth, back * value, back * key]
    sums = [dot_nn(term.astype(BF), tokens).T for term in terms]
    summed = reduce_tokens(reduce_groups(jnp.concatenate(sums, axis=1)))
    return gated, summed


def per_device(inputs, grad_out, w_in, filter_real, filter_imag):
    ctx_count = lax.axis_size("ctx")
    group_count = lax.axis_size("dp")
    tokens = inputs[0]
    cotangent = grad_out[0]
    tok_rows, chan_total = tokens.shape
    chan_half = chan_total // 2
    n_one = filter_real.shape[0] * ctx_count
    n_two = filter_real.shape[1]
    filters = filter_real.shape[2]
    repeats = chan_half // filters
    seq_len = n_one * n_two // 2
    shard_rows = tok_rows // n_two
    per_device_chan = chan_half // ctx_count
    quarter = filter_real.shape[0] // group_count
    use_kernels = (
        per_device_chan % 16 == 0 and quarter % 16 == 0 and repeats % (per_device_chan // 2) == 0
        and ctx_count & (ctx_count - 1) == 0
    )
    chunks = 2 if use_kernels else 1
    rows = 2 * (per_device_chan // chunks)

    tables = tuple(jnp.asarray(table) for table in transform_tables(n_one, n_two))
    order = channel_order(chan_half, filters, ctx_count, chunks)
    pick_np = np.zeros((chan_total, chan_total), np.float32)
    pick_np[np.arange(chan_total), order] = 1.0
    pick = jnp.asarray(pick_np.astype(ml_dtypes.bfloat16))
    group_pos = lax.axis_index("dp")
    arrays = (tokens, cotangent, w_in, filter_real, filter_imag)
    if use_kernels:
        gated, summed = with_kernels(
            arrays, tables, pick, chunks, repeats, group_pos
        )
    else:
        gated, summed = without_kernels(
            arrays, tables, pick, rows, repeats, group_pos
        )

    scale = 1.0 / math.sqrt(inputs.shape[0] * group_count * seq_len)

    ordered = jnp.dot(
        summed.reshape(-1, chan_total), pick.astype(F32), precision=lax.Precision.HIGHEST
    )
    summed = ordered.reshape(summed.shape)
    return (gated[None], summed * scale)


def solution(mesh):
    placed = (
        P("dp", "ctx", None),
        P("dp", "ctx", None),
        P(),
        P("ctx", None, None),
        P("ctx", None, None),
    )
    return jax.shard_map(
        per_device,
        mesh=mesh,
        in_specs=placed,
        out_specs=(P("dp", "ctx", None), P("dp", None)),
        check_vma=False,
    )
```
